128 devices in a mesh: dp: 2 (over core), sp: 64 (over x, y, z).
Axes of the slice: x: 4, y: 4, z: 4, core: 2. Of those that a mesh axis runs over, the one named last changes fastest.
Arguments:
- latents: bfloat16 [256, 64, 64, 128], P(('dp', 'sp')), may hold values from -6 to 6
- cotangent: bfloat16 [256, 64, 64, 128], P(('dp', 'sp')), may hold values from -6 to 6
- frame_counts: int32 [2, 64], P('dp'), may hold values from 1 to 2, as said below
- spatial_weight: bfloat16 [3, 3, 128, 128], replicated, may hold values from -0.1875 to 0.1875
- temporal_weight: bfloat16 [3, 128, 128], replicated, may hold values from -0.3125 to 0.3125
Outputs:
- block_out: bfloat16 [256, 64, 64, 128], P(('dp', 'sp'))
- input_grad: bfloat16 [256, 64, 64, 128], P(('dp', 'sp'))
- spatial_grad: float32 [3, 3, 128, 128], replicated
- temporal_grad: float32 [3, 128, 128], replicated
The draws below stay inside these ranges and needn't reach their ends.
Inputs may be any that keep to these rules, and one draw needn't show every extreme that they name: `frame_counts`: in each group every device holds 1 or 2 frames and the counts sum to 72; in each group some devices hold 2.
All inputs are finite; a program needn't handle non-finite values.
Results may differ from the reference program's by a relative error of at most 0.0054.
Values may be sent and summed in bfloat16 or wider, within the bound.
No kernel may reach another device: no remote copies, remote signals or barrier semaphores. Data moves between devices by JAX's collectives and lax.ppermute only.
A program may use at most 192 MiB of HBM per device.

```python
import jax
import jax.numpy as jnp
from jax import lax

CH = 128
FRAMES = 9
SLOTS = 2
WIDTH = 64
HEIGHT = 64
CLIPS = 8
GROUP_FRAMES = 72
N_DP = 2
N_SP = 64


def draw_frame_counts(key, part):
    key = jax.random.fold_in(key, 5)
    keys = jax.random.split(key, N_DP)
    orders = jax.vmap(lambda single: jax.random.permutation(single, N_SP))(keys)
    return (1 + (orders < CLIPS * FRAMES - N_SP).astype(jnp.int32)).astype(jnp.int32)


def block_levels(stream_key, dims, cuts, least, largest):
    def one(axis_at, parts):
        steps = jax.random.uniform(jax.random.fold_in(jax.random.fold_in(stream_key, 6), axis_at), (parts,), jnp.float32, least / len(cuts), largest / len(cuts))
        return jnp.repeat(jnp.exp(steps), dims[axis_at] // parts).reshape((-1,) + (1,) * (len(dims) - axis_at - 1))

    gain = one(*cuts[0])
    for cut in cuts[1:]:
        gain = gain * one(*cut)
    return gain


def normal_values(own_key, extent, spread, limit, cuts=(), kind=jnp.bfloat16):
    drawn = spread * jax.random.normal(own_key, extent, jnp.float32)
    if cuts:
        drawn = drawn * block_levels(own_key, extent, cuts, -0.22, 0.18)
    return jnp.clip(drawn, -limit, limit).astype(kind)


def setup_inputs(seed: int = 0) -> dict:
    streams_of = jax.random.split(jax.random.key(seed), 6)
    return {
        "latents": normal_values(streams_of[0], (N_DP * N_SP * SLOTS, HEIGHT, WIDTH, CH), 1.0, 6.0, ((0, 128),)),
        "cotangent": normal_values(streams_of[1], (N_DP * N_SP * SLOTS, HEIGHT, WIDTH, CH), 1.0, 6.0, ((0, 128),)),
        "frame_counts": draw_frame_counts(jax.random.fold_in(streams_of[5], 71), 0),
        "spatial_weight": normal_values(streams_of[3], (3, 3, CH, CH), (9 * CH) ** -0.5, 0.1875),
        "temporal_weight": normal_values(streams_of[4], (3, CH, CH), (3 * CH) ** -0.5, 0.3125),
    }


def spatial_apply(padded, kernel, rows, cols):
    total = jnp.zeros(padded.shape[:1] + (rows, cols, kernel.shape[3]), jnp.float32)
    for row_tap in range(3):
        for col_tap in range(3):
            window = padded[:, row_tap:row_tap + rows, col_tap:col_tap + cols].astype(jnp.float32)
            total = total + jnp.einsum('fhwc,cd->fhwd', window, kernel[row_tap, col_tap].astype(jnp.float32))
    return total

def spatial_weights_grad(padded, upstream, rows, cols):
    grads = []
    for row_tap in range(3):
        for col_tap in range(3):
            window = padded[:, row_tap:row_tap + rows, col_tap:col_tap + cols].astype(jnp.float32)
            grads.append(jnp.einsum('fhwc,fhwd->cd', window, upstream.astype(jnp.float32)))
    return jnp.stack(grads).reshape(3, 3, upstream.shape[3], upstream.shape[3])

def temporal_forward(frames, kernel):
    nclip = frames.shape[0] // FRAMES
    blocks = frames.reshape(nclip, FRAMES, -1, frames.shape[3]).astype(jnp.float32)
    padded = jnp.pad(blocks, ((0, 0), (2, 0), (0, 0), (0, 0)))
    total = jnp.zeros(blocks.shape, jnp.float32)
    for tap_index in range(3):
        total = total + jnp.einsum('cfpd,de->cfpe', padded[:, 2 - tap_index:2 - tap_index + FRAMES], kernel[tap_index].astype(jnp.float32))
    return total.reshape(frames.shape)

def temporal_backward(grads, kernel):
    nclip = grads.shape[0] // FRAMES
    blocks = grads.reshape(nclip, FRAMES, -1, grads.shape[3]).astype(jnp.float32)
    padded = jnp.pad(blocks, ((0, 0), (0, 2), (0, 0), (0, 0)))
    total = jnp.zeros(blocks.shape, jnp.float32)
    for tap_index in range(3):
        total = total + jnp.einsum('cfpe,de->cfpd', padded[:, tap_index:tap_index + FRAMES], kernel[tap_index].astype(jnp.float32))
    return total.reshape(grads.shape)

def temporal_weights_grad(frames, grads):
    nclip = frames.shape[0] // FRAMES
    blocks = frames.reshape(nclip, FRAMES, -1, frames.shape[3]).astype(jnp.float32)
    gblocks = grads.reshape(nclip, FRAMES, -1, grads.shape[3]).astype(jnp.float32)
    padded = jnp.pad(blocks, ((0, 0), (2, 0), (0, 0), (0, 0)))
    result = []
    for tap_index in range(3):
        result.append(jnp.einsum('cfpd,cfpe->de', padded[:, 2 - tap_index:2 - tap_index + FRAMES], gblocks))
    return jnp.stack(result)

def frame_index(counts_row, slots, nframes):
    sp_count = counts_row.shape[0]
    starts = (jnp.cumsum(counts_row) - counts_row).astype(jnp.int32)
    frame_ids = jnp.arange(nframes, dtype=jnp.int32)
    holder = (lax.optimization_barrier(jnp.sum((starts[None, :] <= frame_ids[:, None]).astype(jnp.int32), axis=1)) - 1).astype(jnp.int32)
    first_frame = lax.optimization_barrier(jnp.sum(jnp.where(jnp.arange(sp_count, dtype=jnp.int32)[None, :] == holder[:, None], starts[None, :], 0), axis=1))
    return (holder * slots + frame_ids - first_frame).astype(jnp.int32)

def slot_layout(counts_row, slots):
    starts = (jnp.cumsum(counts_row) - counts_row).astype(jnp.int32)
    offset = jnp.arange(counts_row.shape[0] * slots, dtype=jnp.int32) % slots
    slot_frame = (jnp.repeat(starts, slots) + offset).astype(jnp.int32)
    is_live = offset < jnp.repeat(counts_row, slots)
    return (slot_frame, is_live)

def to_slots(frames, slot_frame, is_live):
    picked = jnp.take(frames, jnp.clip(slot_frame, 0, frames.shape[0] - 1), axis=0)
    return jnp.where(is_live[:, None, None, None], picked, jnp.zeros_like(picked))

def reference(latents, cotangent, frame_counts, spatial_weight, temporal_weight):
    per_group = N_SP * SLOTS
    flipped = jnp.transpose(spatial_weight[::-1, ::-1], (0, 1, 3, 2))
    outs, igrads = ([], [])
    spatial_sum = jnp.zeros((3, 3, CH, CH), jnp.float32)
    temporal_sum = jnp.zeros((3, CH, CH), jnp.float32)
    for group in range(N_DP):
        counts_row = frame_counts[group]
        index = frame_index(counts_row, SLOTS, GROUP_FRAMES)
        inputs = jnp.take(latents[group * per_group:(group + 1) * per_group], index, axis=0)
        grads = jnp.take(cotangent[group * per_group:(group + 1) * per_group], index, axis=0)
        wide = inputs.astype(jnp.float32)
        activated = jax.nn.silu(wide).astype(jnp.bfloat16)
        act_pad = jnp.pad(activated, ((0, 0), (1, 1), (1, 1), (0, 0)))
        spatial_out = spatial_apply(act_pad, spatial_weight, HEIGHT, WIDTH).astype(jnp.bfloat16)
        temporal_out = temporal_forward(spatial_out, temporal_weight).astype(jnp.bfloat16)
        result = (wide + temporal_out.astype(jnp.float32)).astype(jnp.bfloat16)
        upstream = temporal_backward(grads, temporal_weight).astype(jnp.bfloat16)
        temporal_sum = temporal_sum + temporal_weights_grad(spatial_out, grads)
        up_pad = jnp.pad(upstream, ((0, 0), (1, 1), (1, 1), (0, 0)))
        back_spatial = spatial_apply(up_pad, flipped, HEIGHT, WIDTH)
        sig = jax.nn.sigmoid(wide)
        in_grad = (grads.astype(jnp.float32) + back_spatial * sig * (1.0 + wide * (1.0 - sig))).astype(jnp.bfloat16)
        spatial_sum = spatial_sum + spatial_weights_grad(act_pad, upstream, HEIGHT, WIDTH)
        slot_frame, is_live = slot_layout(counts_row, SLOTS)
        outs.append(to_slots(result, slot_frame, is_live))
        igrads.append(to_slots(in_grad, slot_frame, is_live))
    scale = float(N_DP * GROUP_FRAMES * HEIGHT * WIDTH) ** (-0.5)
    return (jnp.concatenate(outs, axis=0), jnp.concatenate(igrads, axis=0), spatial_sum * scale, temporal_sum * scale)
```

```python
import functools

import jax
import jax.numpy as jnp
from jax import lax
from jax.experimental import pallas as pl
from jax.experimental.pallas import tpu as pltpu
from jax.sharding import PartitionSpec as P

FRAMES = 9
CH = 128
ROWS = 64
COLS = 64
PAIRS = ROWS // 2
BLK = 8
NBLK = PAIRS // BLK
PX = BLK * COLS
F32 = jnp.float32
BF16 = jnp.bfloat16
VMEM_BYTES = 48 * 1024 * 1024


def dot(a, b):
    return jnp.dot(a, b, preferred_element_type=F32)


def dot_t(a, b):
    return lax.dot_general(a, b, (((0,), (0,)), ((), ())), preferred_element_type=F32)


def clear_edges(wide):
    wide[0, :, 0 : 3 * CH] = jnp.zeros((COLS, 3 * CH), BF16)
    wide[PAIRS, :, 3 * CH : 6 * CH] = jnp.zeros((COLS, 3 * CH), BF16)


def put_row(wide, t, half, a):
    col = lax.broadcasted_iota(jnp.int32, a.shape, 1)
    before = jnp.where(col == 0, 0.0, pltpu.roll(a, 1, 1))
    after = jnp.where(col == COLS - 1, 0.0, pltpu.roll(a, COLS - 1, 1))
    at = pl.ds(t + half, BLK)
    base = 0 if half else 3 * CH
    wide[at, :, base : base + CH] = before.astype(BF16)
    wide[at, :, base + CH : base + 2 * CH] = a.astype(BF16)
    wide[at, :, base + 2 * CH : base + 3 * CH] = after.astype(BF16)


def silu(x):
    return x * jax.nn.sigmoid(x)


def fill_act(wide, x_ref):
    clear_edges(wide)

    def body(n, _):
        t = n * BLK
        for half in range(2):
            put_row(wide, t, half, silu(x_ref[pl.ds(t, BLK), half].astype(F32)))
        return 0

    lax.fori_loop(0, NBLK, body, 0)


def windows(wide, t):
    low = wide[pl.ds(t, BLK)].reshape(PX, 6 * CH)
    high = wide[pl.ds(t + 1, BLK)].reshape(PX, 6 * CH)
    return low, high


def conv(wide, w_ref, t):
    low, high = windows(wide, t)
    return dot(low, w_ref[0 : 6 * CH, :]) + dot(high, w_ref[6 * CH : 12 * CH, :])


def conv_to(out_ref, wide, w_ref):
    def body(n, _):
        t = n * BLK
        out_ref[pl.ds(t, BLK)] = conv(wide, w_ref, t).astype(BF16).reshape(BLK, COLS, 2 * CH)
        return 0

    lax.fori_loop(0, NBLK, body, 0)


def pair(ref, t):
    v = ref[pl.ds(t, BLK)]
    return jnp.concatenate([v[:, 0], v[:, 1]], axis=-1).reshape(PX, 2 * CH)


def flat(ref, t):
    return ref[pl.ds(t, BLK)].reshape(PX, 2 * CH)


def frame_spec(lead=()):
    return lead + (PAIRS, 2, COLS, CH)


def forward_kernel(info, x_ref, w_ref, s_ref, wide):
    fill_act(wide, x_ref.at[0])
    conv_to(s_ref.at[0], wide, w_ref)

    @pl.when(info[0] == 2)
    def _():
        fill_act(wide, x_ref.at[1])
        conv_to(s_ref.at[1], wide, w_ref)


def grad_kernel(info, x_ref, g_ref, xh_ref, gn_ref, s_ref, w_ref, tw_ref, out_ref, sh_ref, wide, gsel, vw, acc, tacc, *, scale):
    two = info[0] == 2
    acc[...] = jnp.zeros_like(acc)
    tacc[...] = jnp.zeros_like(tacc)
    def choose(n, _):
        t = n * BLK
        gsel[pl.ds(t, BLK)] = jnp.where(two, g_ref[1, pl.ds(t, BLK)], gn_ref[pl.ds(t, BLK)])
        return 0

    lax.fori_loop(0, NBLK, choose, 0)

    def masked(k, keep):
        vw[k] = jnp.where(keep, tw_ref[k], jnp.zeros_like(tw_ref[k]))

    def add_spatial(value, t):
        low, high = windows(wide, t)
        v = value.astype(BF16)
        acc[:, 0 : 6 * CH] += dot_t(v, low)
        acc[:, 6 * CH : 12 * CH] += dot_t(v, high)

    def add_temporal(s0, s1, g0, g1, keep0, keep1, t):
        for half in range(2):
            lanes = slice(half * CH, half * CH + CH)
            a0 = s0[pl.ds(t, BLK), :, lanes].reshape(PX, CH)
            a1 = s1[pl.ds(t, BLK), :, lanes].reshape(PX, CH)
            b0 = g0[pl.ds(t, BLK), half].reshape(PX, CH)
            b1 = g1[pl.ds(t, BLK), half].reshape(PX, CH)
            a1 = jnp.where(keep0, a1, jnp.zeros_like(a1))
            b1 = jnp.where(keep1, b1, jnp.zeros_like(b1))
            tacc[...] += dot_t(jnp.concatenate([a0, a1], -1), jnp.concatenate([b0, b1], -1))

    before, after0, after1, after2 = (info[k] == 1 for k in range(1, 5))

    fill_act(wide, xh_ref)
    conv_to(sh_ref, wide, w_ref)
    masked(2, jnp.logical_and(before, after0))

    def from_halo(n, _):
        t = n * BLK
        add_spatial(dot(pair(gsel, t), vw[2]), t)
        add_temporal(s_ref.at[0], sh_ref, g_ref.at[0], gsel, before, after0, t)
        return 0

    lax.fori_loop(0, NBLK, from_halo, 0)

    fill_act(wide, x_ref.at[0])
    masked(1, after0)
    masked(2, jnp.logical_and(two, after1))

    def from_first(n, _):
        t = n * BLK
        value = dot(pair(g_ref.at[0], t), tw_ref[0]) + dot(pair(gsel, t), vw[1]) + dot(pair(gn_ref, t), vw[2])
        add_spatial(value, t)
        return 0

    lax.fori_loop(0, NBLK, from_first, 0)

    @pl.when(two)
    def _():
        fill_act(wide, x_ref.at[1])
        masked(1, after2)

        def from_second(n, _):
            t = n * BLK
            value = dot(pair(g_ref.at[1], t), tw_ref[0]) + dot(pair(gn_ref, t), vw[1])
            add_spatial(value, t)
            add_temporal(s_ref.at[1], s_ref.at[0], g_ref.at[1], gn_ref, after0, after2, t)
            return 0

        lax.fori_loop(0, NBLK, from_second, 0)

    for p in range(3):
        for q in range(3):
            first = (p * 3 + q) * CH
            second = ((p + 1) * 3 + q) * CH
            both = acc[0:CH, first : first + CH] + acc[CH : 2 * CH, second : second + CH]
            out_ref[p * 3 + q] = both.T * scale
    out_ref[9] = tacc[0:CH, 0:CH] * scale
    out_ref[10] = tacc[0:CH, CH : 2 * CH] * scale
    out_ref[11] = tacc[CH : 2 * CH, CH : 2 * CH] * scale


def output_kernel(info, x_ref, s_ref, sh_ref, xh_ref, w_ref, tw_ref, out_ref, wide, s2, mw):
    fill_act(wide, xh_ref)
    conv_to(s2, wide, w_ref)

    def slot(j, here, back1, back2, keep1, keep2):
        mw[0] = jnp.where(keep1, tw_ref[1], jnp.zeros_like(tw_ref[1]))
        mw[1] = jnp.where(keep2, tw_ref[2], jnp.zeros_like(tw_ref[2]))

        def body(n, _):
            t = n * BLK
            value = dot(flat(here, t), tw_ref[0]) + dot(flat(back1, t), mw[0]) + dot(flat(back2, t), mw[1])
            value = value.astype(BF16).astype(F32).reshape(BLK, COLS, 2 * CH)
            for half in range(2):
                wide_x = x_ref[j, pl.ds(t, BLK), half].astype(F32)
                out_ref[j, pl.ds(t, BLK), half] = (wide_x + value[:, :, half * CH : half * CH + CH]).astype(BF16)
            return 0

        lax.fori_loop(0, NBLK, body, 0)

    slot(0, s_ref.at[0], sh_ref, s2, info[1] == 1, info[2] == 1)

    @pl.when(info[0] == 2)
    def _():
        slot(1, s_ref.at[1], s_ref.at[0], sh_ref, info[3] == 1, info[4] == 1)

    @pl.when(info[0] != 2)
    def _():
        out_ref[1] = jnp.zeros_like(out_ref[1])


def input_kernel(info, x_ref, g_ref, gn_ref, gnn_ref, w_ref, tw_ref, out_ref, wide, mw):
    two = info[0] == 2

    def slot(j, next1, next2, keep1, keep2):
        mw[0] = jnp.where(keep1, tw_ref[1], jnp.zeros_like(tw_ref[1]))
        mw[1] = jnp.where(keep2, tw_ref[2], jnp.zeros_like(tw_ref[2]))
        clear_edges(wide)

        def up(n, _):
            t = n * BLK
            value = dot(pair(g_ref.at[j], t), tw_ref[0]) + dot(next1(t), mw[0]) + dot(next2(t), mw[1])
            value = value.reshape(BLK, COLS, 2 * CH)
            for half in range(2):
                put_row(wide, t, half, value[:, :, half * CH : half * CH + CH])
            return 0

        lax.fori_loop(0, NBLK, up, 0)

        def down(n, _):
            t = n * BLK
            back = conv(wide, w_ref, t).reshape(BLK, COLS, 2 * CH)
            for half in range(2):
                x = x_ref[j, pl.ds(t, BLK), half].astype(F32)
                g = g_ref[j, pl.ds(t, BLK), half].astype(F32)
                sig = jax.nn.sigmoid(x)
                b = back[:, :, half * CH : half * CH + CH]
                out_ref[j, pl.ds(t, BLK), half] = (g + b * (sig * (1.0 + x * (1.0 - sig)))).astype(BF16)
            return 0

        lax.fori_loop(0, NBLK, down, 0)

    slot(
        0,
        lambda t: jnp.where(two, pair(g_ref.at[1], t), pair(gn_ref, t)),
        lambda t: jnp.where(two, pair(gn_ref, t), pair(gnn_ref, t)),
        info[1] == 1,
        info[2] == 1,
    )

    @pl.when(two)
    def _():
        slot(1, lambda t: pair(gn_ref, t), lambda t: pair(gnn_ref, t), info[3] == 1, info[4] == 1)

    @pl.when(info[0] != 2)
    def _():
        out_ref[1] = jnp.zeros_like(out_ref[1])


WIDE = pltpu.VMEM((PAIRS + 1, COLS, 6 * CH), BF16)
SMEM = pl.BlockSpec(memory_space=pltpu.SMEM)
VMEM = pl.BlockSpec(memory_space=pltpu.VMEM)


def call(kernel, n_in, outs, scratch, name):
    return pl.pallas_call(
        kernel,
        in_specs=[SMEM] + [VMEM] * n_in,
        out_specs=[VMEM] * len(outs),
        out_shape=[jax.ShapeDtypeStruct(s, d) for s, d in outs],
        scratch_shapes=scratch,
        compiler_params=pltpu.CompilerParams(vmem_limit_bytes=VMEM_BYTES),
        name=name,
    )


S_SHAPE = (PAIRS, COLS, 2 * CH)


def forward(info, x, w):
    return call(forward_kernel, 2, [((2,) + S_SHAPE, BF16)], [WIDE], "forward")(info, x, w)[0]


def grads(info, x, g, xh, gn, s, w, tw, scale):
    scratch = [
        WIDE,
        pltpu.VMEM((PAIRS, 2, COLS, CH), BF16),
        pltpu.VMEM((3, 2 * CH, 2 * CH), BF16),
        pltpu.VMEM((2 * CH, 12 * CH), F32),
        pltpu.VMEM((2 * CH, 2 * CH), F32),
    ]
    outs = [((12, CH, CH), F32), (S_SHAPE, BF16)]
    return call(functools.partial(grad_kernel, scale=scale), 7, outs, scratch, "grads")(info, x, g, xh, gn, s, w, tw)


def output(info, x, s, sh, xh, w, tw):
    scratch = [WIDE, pltpu.VMEM(S_SHAPE, BF16), pltpu.VMEM((2, 2 * CH, 2 * CH), BF16)]
    return call(output_kernel, 6, [(frame_spec((2,)), BF16)], scratch, "output")(info, x, s, sh, xh, w, tw)[0]


def input_grads(info, x, g, gn, gnn, w, tw):
    scratch = [WIDE, pltpu.VMEM((2, 2 * CH, 2 * CH), BF16)]
    return call(input_kernel, 6, [(frame_spec((2,)), BF16)], scratch, "input_grads")(info, x, g, gn, gnn, w, tw)[0]


def pair_weight(w):
    zero = jnp.zeros((1, 3, CH, CH), w.dtype)
    first = jnp.concatenate([w, zero], 0).reshape(12 * CH, CH)
    second = jnp.concatenate([zero, w], 0).reshape(12 * CH, CH)
    return jnp.concatenate([first, second], 1)


def twice(w):
    zero = jnp.zeros_like(w)
    return jnp.concatenate([jnp.concatenate([w, zero], 2), jnp.concatenate([zero, w], 2)], 1)


def total(part, sp_count):
    core = lax.axis_index("dp")
    swap = [(0, 1), (1, 0)]
    halves = part.reshape(2, 6 * CH, CH)
    own = lax.dynamic_index_in_dim(halves, core, 0, keepdims=False)
    other = lax.dynamic_index_in_dim(halves, 1 - core, 0, keepdims=False)
    own = own + lax.ppermute(other, "dp", swap)
    rows = 6 * CH // sp_count
    pieces = lax.all_to_all(own.reshape(sp_count, rows, CH), "sp", 0, 0, tiled=True)
    piece = jnp.sum(pieces, axis=0)
    spread = lax.all_to_all(jnp.broadcast_to(piece[None], (sp_count, rows, CH)), "sp", 0, 0, tiled=True)
    mine = spread.reshape(6 * CH, CH)
    theirs = lax.ppermute(mine, "dp", swap)
    both = jnp.where(core == 0, jnp.stack([mine, theirs]), jnp.stack([theirs, mine]))
    return both.reshape(12, CH, CH)


def local(latents, cotangent, frame_counts, spatial_weight, temporal_weight):
    sp_count = lax.axis_size("sp")
    nframes = sp_count // 8 * FRAMES
    scale = float(lax.axis_size("dp") * nframes * ROWS * COLS) ** (-0.5)
    counts = frame_counts[0]
    here = lax.axis_index("sp")
    order = jnp.arange(sp_count, dtype=jnp.int32)
    count = jnp.sum(jnp.where(order == here, counts, 0))
    place = jnp.sum(jnp.where(order < here, counts, 0)) % FRAMES
    place1 = (place + 1) % FRAMES
    two = count == 2

    def flags(*conditions):
        return jnp.stack([count] + [c.astype(jnp.int32) for c in conditions])

    x = latents.reshape(2, PAIRS, 2, COLS, CH)
    g = cotangent.reshape(2, PAIRS, 2, COLS, CH)
    low = [(i, i + 1) for i in range(0, sp_count, 2)] + [(i + 1, i) for i in range(0, sp_count, 2)]
    high = [(i, (i + 1) % sp_count) for i in range(1, sp_count, 2)] + [((i + 1) % sp_count, i) for i in range(1, sp_count, 2)]
    even = here % 2 == 0

    def exchange(up, down):
        from_high = lax.ppermute(jnp.where(even, down, up), "sp", high)
        from_low = lax.ppermute(jnp.where(even, up, down), "sp", low)
        return jnp.where(even, from_high, from_low), jnp.where(even, from_low, from_high)

    x_last = jnp.where(two, x[1], x[0])
    xh, gn = exchange(x_last, g[0])
    xhh, gnn = exchange(jnp.where(two, x[0], xh), jnp.where(two, g[1], gn))

    w_fwd = pair_weight(spatial_weight)
    w_bwd = pair_weight(jnp.transpose(spatial_weight[::-1, ::-1], (0, 1, 3, 2)))
    tw_fwd = twice(temporal_weight)
    tw_bwd = twice(jnp.swapaxes(temporal_weight, 1, 2))

    s = forward(flags(), x, w_fwd)
    last = FRAMES - 1
    part, sh = grads(
        flags(place >= 1, place + 1 <= last, place + 2 <= last, place1 + 1 <= last),
        x, g, xh, gn, s, w_fwd, tw_bwd, scale,
    )
    summed = total(part, sp_count)
    block_out = output(flags(place >= 1, place >= 2, place1 >= 1, place1 >= 2), x, s, sh, xhh, w_fwd, tw_fwd)
    input_grad = input_grads(
        flags(place + 1 <= last, place + 2 <= last, place1 + 1 <= last, place1 + 2 <= last),
        x, g, gn, gnn, w_bwd, tw_bwd,
    )
    return (
        block_out.reshape(latents.shape),
        input_grad.reshape(latents.shape),
        summed[:9].reshape(3, 3, CH, CH),
        summed[9:],
    )


def solution(mesh):
    return jax.shard_map(
        local,
        mesh=mesh,
        in_specs=(
            P(("dp", "sp"), None, None, None),
            P(("dp", "sp"), None, None, None),
            P("dp", None),
            P(),
            P(),
        ),
        out_specs=(P(("dp", "sp"), None, None, None), P(("dp", "sp"), None, None, None), P(), P()),
        check_vma=False,
    )
```

```python
import functools

import jax
import jax.numpy as jnp
from jax import lax
from jax.experimental import pallas as pl
from jax.experimental.pallas import tpu as pltpu
from jax.sharding import Mesh
from jax.sharding import PartitionSpec as P

FRAMES = 9
CLIPS = 8
CH = 128
ROWS = 64
COLS = 64
N_SP = 64
SIDE = 4
PAIRS = ROWS // 2
F32 = jnp.float32
BF16 = jnp.bfloat16
VMEM_BYTES = 32 * 1024 * 1024
SCALE = float(2 * CLIPS * FRAMES * ROWS * COLS) ** (-0.5)
HALF = 6 * CH
PIECE = HALF // (SIDE * SIDE)

COUNT, EVEN, BACK1, BACK2, NEXT1, NEXT2, LBACK1, LBACK2, LNEXT1, LNEXT2, CORE, AT_X, AT_Y = range(13)
INFO = 16

FILL = 8
MID = 16
FULL = 32


def dot(a, b):
    return jnp.dot(a, b, preferred_element_type=F32)


def dot_t(a, b):
    return lax.dot_general(a, b, (((0,), (0,)), ((), ())), preferred_element_type=F32)


def steps(block, body):
    def one(n, _):
        body(n * block)
        return 0

    lax.fori_loop(0, PAIRS // block, one, 0)


def clear_edges(wide):
    wide[0, :, 0 : 3 * CH] = jnp.zeros((COLS, 3 * CH), BF16)
    wide[PAIRS, :, 3 * CH : 6 * CH] = jnp.zeros((COLS, 3 * CH), BF16)


def put_row(wide, t, half, a):
    col = lax.broadcasted_iota(jnp.int32, a.shape, 1)
    before = jnp.where(col == 0, 0.0, pltpu.roll(a, 1, 1))
    after = jnp.where(col == COLS - 1, 0.0, pltpu.roll(a, COLS - 1, 1))
    at = pl.ds(t + half, a.shape[0])
    base = 0 if half else 3 * CH
    wide[at, :, base : base + CH] = before.astype(BF16)
    wide[at, :, base + CH : base + 2 * CH] = a.astype(BF16)
    wide[at, :, base + 2 * CH : base + 3 * CH] = after.astype(BF16)


def fill_act(wide, rows):
    def body(t):
        for half in range(2):
            x = rows(t, half).astype(F32)
            put_row(wide, t, half, x * jax.nn.sigmoid(x))

    steps(FILL, body)


def windows(wide, t, block):
    low = wide[pl.ds(t, block)].reshape(block * COLS, 6 * CH)
    high = wide[pl.ds(t + 1, block)].reshape(block * COLS, 6 * CH)
    return low, high


def conv(wide, w_ref, t, block):
    low, high = windows(wide, t, block)
    return dot(low, w_ref[0 : 6 * CH, :]) + dot(high, w_ref[6 * CH : 12 * CH, :])


def conv_to(out_ref, wide, w_ref):
    def body(t):
        out_ref[pl.ds(t, FULL)] = conv(wide, w_ref, t, FULL).astype(BF16).reshape(FULL, COLS, 2 * CH)

    steps(FULL, body)


def pair(v):
    return jnp.concatenate([v[:, 0], v[:, 1]], axis=-1).reshape(v.shape[0] * COLS, 2 * CH)


def flat(v):
    return v.reshape(v.shape[0] * COLS, 2 * CH)


def add_spatial(acc, wide, v_ref):
    def body(t):
        low, high = windows(wide, t, FULL)
        v = flat(v_ref[pl.ds(t, FULL)])
        acc[:, 0 : 6 * CH] += dot_t(v, low)
        acc[:, 6 * CH : 12 * CH] += dot_t(v, high)

    steps(FULL, body)


def correlate(s, gs):
    total = None
    for half in range(2):
        a = s[:, :, half * CH : half * CH + CH].reshape(PAIRS * COLS, CH)
        b = gs(half)
        one = dot_t(a, b.reshape(PAIRS * COLS, b.shape[-1]))
        total = one if total is None else total + one
    return total


def begin(copies, sems):
    found = [pltpu.make_async_copy(a, b, sems.at[n]) for n, (a, b) in enumerate(copies)]
    for c in found:
        c.start()
    return found


def begin_either(first, a, b, target, sem):
    @pl.when(first)
    def _():
        pltpu.make_async_copy(a, target, sem).start()

    @pl.when(jnp.logical_not(first))
    def _():
        pltpu.make_async_copy(b, target, sem).start()

    return pltpu.make_async_copy(a, target, sem)


def prep_kernel(counts, place, x_ref, g_ref, info, high_ref, low_ref, sems):
    here = place[0]

    def add(n, carry):
        total, own = carry
        c = counts[0, n]
        return total + jnp.where(n < here, c, 0), own + jnp.where(n == here, c, 0)

    start, count = lax.fori_loop(0, N_SP, add, (jnp.int32(0), jnp.int32(0)), unroll=8)
    first = start % FRAMES
    second = (first + 1) % FRAMES
    final = FRAMES - 1
    even = here % 2 == 0
    values = {
        COUNT: count,
        EVEN: even.astype(jnp.int32),
        BACK1: (first >= 1).astype(jnp.int32),
        BACK2: (first >= 2).astype(jnp.int32),
        NEXT1: (first + 1 <= final).astype(jnp.int32),
        NEXT2: (first + 2 <= final).astype(jnp.int32),
        LBACK1: (second >= 1).astype(jnp.int32),
        LBACK2: (second >= 2).astype(jnp.int32),
        LNEXT1: (second + 1 <= final).astype(jnp.int32),
        LNEXT2: (second + 2 <= final).astype(jnp.int32),
        CORE: place[1],
        AT_X: here // (SIDE * SIDE),
        AT_Y: (here // SIDE) % SIDE,
    }
    for at, value in values.items():
        info[at] = value
    for at in range(len(values), INFO):
        info[at] = 0
    last = jnp.where(count == 2, 1, 0)

    def send(up_ref, down_ref):
        up = pltpu.make_async_copy(x_ref.at[last], up_ref, sems.at[0])
        down = pltpu.make_async_copy(g_ref.at[0], down_ref, sems.at[1])
        up.start()
        down.start()
        up.wait()
        down.wait()

    @pl.when(even)
    def _():
        send(low_ref, high_ref)

    @pl.when(jnp.logical_not(even))
    def _():
        send(high_ref, low_ref)


def forward_kernel(
    info, x_any, g_any, w_any, tw_any, s_ref, acc, tacc, wf, wb, tf, tb, wide, v_ref, mw, x_ref, g_ref, w_ref, tw_ref, sems
):
    need_w, need_tw, need_x, need_g = begin([(w_any, w_ref), (tw_any, tw_ref), (x_any, x_ref), (g_any, g_ref)], sems)
    need_w.wait()
    need_tw.wait()
    zero = jnp.zeros((CH, CH), BF16)
    for a in range(4):
        for q in range(3):
            rows = slice((a * 3 + q) * CH, (a * 3 + q + 1) * CH)
            for b in range(2):
                lanes = slice(b * CH, b * CH + CH)
                inside = 0 <= a - b <= 2
                wf[rows, lanes] = w_ref[a - b, q] if inside else zero
                wb[rows, lanes] = w_ref[2 - (a - b), 2 - q].T if inside else zero
    for k in range(3):
        for a in range(2):
            rows = slice((2 * k + a) * CH, (2 * k + a + 1) * CH)
            for b in range(2):
                lanes = slice(b * CH, b * CH + CH)
                tf[rows, lanes] = tw_ref[k] if a == b else zero
                tb[rows, lanes] = tw_ref[k].T if a == b else zero

    acc[...] = jnp.zeros_like(acc)
    tacc[...] = jnp.zeros_like(tacc)
    clear_edges(wide)
    mw[0 : 2 * CH] = tb[0 : 2 * CH]
    need_x.wait()
    need_g.wait()

    def slot(j, _):
        keep = jnp.logical_and(j == 0, jnp.logical_and(info[COUNT] == 2, info[NEXT1] == 1))
        mw[2 * CH : 4 * CH] = jnp.where(keep, tb[2 * CH : 4 * CH], jnp.zeros((2 * CH, 2 * CH), BF16))
        fill_act(wide, lambda t, half: x_ref[j, pl.ds(t, FILL), half])
        conv_to(s_ref.at[j], wide, wf)

        def upstream(t):
            at = pl.ds(t, MID)
            both = jnp.concatenate([pair(g_ref[j, at]), pair(g_ref[1, at])], axis=-1)
            v_ref[at] = dot(both, mw[...]).astype(BF16).reshape(MID, COLS, 2 * CH)

        steps(MID, upstream)
        add_spatial(acc, wide, v_ref)
        found = correlate(s_ref[j], lambda half: jnp.concatenate([g_ref[j, :, half], g_ref[1, :, half]], axis=-1))
        tacc[:, 0:CH] += found[:, 0:CH]
        tacc[:, CH : 2 * CH] += jnp.where(keep, found[:, CH : 2 * CH], 0.0)
        return 0

    lax.fori_loop(0, info[COUNT], slot, 0)


def prep2_kernel(info, x_ref, g_ref, high_in, low_in, after, info_out, high_ref, low_ref, sems):
    for n in range(INFO):
        info_out[n] = info[n]
    two = info[COUNT] == 2
    even = info[EVEN] == 1

    def send(for_high, for_low):
        for c in begin([(for_high, high_ref), (for_low, low_ref)], sems):
            c.wait()

    @pl.when(jnp.logical_not(two))
    def _():
        send(low_in, high_in)

    @pl.when(jnp.logical_and(two, even))
    def _():
        send(g_ref.at[1], x_ref.at[0])

    @pl.when(jnp.logical_and(two, jnp.logical_not(even)))
    def _():
        send(x_ref.at[0], g_ref.at[1])


def grad_kernel(
    info, high_in, low_in, x_any, g_any, s_any, acc_any, tacc_any, wf_any, tb_any, own_ref, other_ref, sh_out,
    wide, xh, gn, x, g, s, v, sh, acc, tacc, wf, tb, mw, both, sems,
):
    two = info[COUNT] == 2
    even = info[EVEN] == 1
    back = info[BACK1] == 1
    cross = jnp.logical_and(back, info[NEXT1] == 1)
    need_x = begin_either(even, high_in, low_in, xh, sems.at[0])
    need = begin(
        [(wf_any, wf), (tb_any, tb), (g_any, g), (acc_any, acc), (tacc_any, tacc), (x_any.at[0], x), (s_any.at[0], s)],
        sems.at[pl.ds(2, 7)],
    )
    need_n = begin_either(even, low_in, high_in, gn, sems.at[1])
    clear_edges(wide)
    need_x.wait()
    fill_act(wide, lambda t, half: xh[pl.ds(t, FILL), half])
    need[0].wait()
    conv_to(sh, wide, wf)
    keep_sh = pltpu.make_async_copy(sh, sh_out, sems.at[9])
    keep_sh.start()
    for c in need[1:3] + [need_n]:
        c.wait()
    nothing = jnp.zeros((2 * CH, 2 * CH), BF16)
    mw[0 : 2 * CH] = jnp.where(back, tb[2 * CH : 4 * CH], nothing)
    mw[2 * CH : 4 * CH] = jnp.where(cross, tb[4 * CH : 6 * CH], nothing)

    def upstream(t):
        at = pl.ds(t, MID)
        u = jnp.concatenate([pair(g[0, at]), pair(jnp.where(two, g[1, at], gn[at]))], axis=-1)
        v[at] = dot(u, mw[...]).astype(BF16).reshape(MID, COLS, 2 * CH)

    steps(MID, upstream)
    for c in need[3:5]:
        c.wait()
    add_spatial(acc, wide, v)

    def two_frames(half):
        return jnp.concatenate([g[0, :, half], jnp.where(two, g[1, :, half], gn[:, half])], axis=-1)

    found = correlate(sh[...], two_frames)
    tacc[:, CH : 2 * CH] += jnp.where(back, found[:, 0:CH], 0.0)
    tacc[:, 2 * CH : 3 * CH] += jnp.where(cross, found[:, CH : 2 * CH], 0.0)
    for c in need[5:] + [keep_sh]:
        c.wait()

    @pl.when(jnp.logical_and(two, info[NEXT2] == 1))
    def _():
        fill_act(wide, lambda t, half: x[pl.ds(t, FILL), half])

        def up(t):
            at = pl.ds(t, MID)
            v[at] = dot(pair(gn[at]), tb[4 * CH : 6 * CH]).astype(BF16).reshape(MID, COLS, 2 * CH)

        steps(MID, up)
        add_spatial(acc, wide, v)
        tacc[:, 2 * CH : 3 * CH] += correlate(s[...], lambda half: gn[:, half])

    at_x, at_y, core = info[AT_X], info[AT_Y], info[CORE]
    for p in range(3):
        for q in range(3):
            first = (p * 3 + q) * CH
            second = ((p + 1) * 3 + q) * CH
            found = acc[0:CH, first : first + CH] + acc[CH : 2 * CH, second : second + CH]
            n = p * 3 + q
            both[n // 6, (n % 6) * CH : (n % 6 + 1) * CH] = found.T * SCALE
    for k in range(3):
        both[1, (3 + k) * CH : (4 + k) * CH] = tacc[:, k * CH : k * CH + CH] * SCALE
    for i in range(SIDE):
        for j in range(SIDE):
            piece = lax.rem(at_x + i, SIDE) * SIDE + lax.rem(at_y + j, SIDE)
            source = pl.ds(pl.multiple_of(piece * PIECE, PIECE), PIECE)
            own_ref[i, j] = both[core, source]
            other_ref[i, j] = both[1 - core, source]


def add_x(x, out, t, value):
    at = pl.ds(t, MID)
    value = value.astype(BF16).astype(F32).reshape(MID, COLS, 2 * CH)
    for half in range(2):
        out[at, half] = (x[at, half].astype(F32) + value[:, :, half * CH : half * CH + CH]).astype(BF16)


def mask_taps(mw, taps, keep1, keep2):
    nothing = jnp.zeros((2 * CH, 2 * CH), BF16)
    mw[0 : 2 * CH] = taps[0 : 2 * CH]
    mw[2 * CH : 4 * CH] = jnp.where(keep1, taps[2 * CH : 4 * CH], nothing)
    mw[4 * CH : 6 * CH] = jnp.where(keep2, taps[4 * CH : 6 * CH], nothing)


def input_rows(wide, wb, upstream, x, g, out, first, count):
    clear_edges(wide)

    def up(t, n):
        value = upstream(t, n).reshape(n, COLS, 2 * CH)
        for half in range(2):
            put_row(wide, t, half, value[:, :, half * CH : half * CH + CH])

    def up_full(n, _):
        up(first + n * FILL, FILL)
        return 0

    lax.fori_loop(0, count // FILL, up_full, 0)
    if first > 0:
        up(first - 1, 1)
    if first + count < PAIRS:
        up(first + count, 1)

    def down(n, _):
        t = first + n * MID
        at = pl.ds(t, MID)
        back = conv(wide, wb, t, MID).reshape(MID, COLS, 2 * CH)
        for half in range(2):
            xv = x[at, half].astype(F32)
            sig = jax.nn.sigmoid(xv)
            b = back[:, :, half * CH : half * CH + CH]
            out[at, half] = (g[at, half].astype(F32) + b * (sig * (1.0 + xv * (1.0 - sig)))).astype(BF16)
        return 0

    lax.fori_loop(0, count // MID, down, 0)


def early_out_kernel(info, x_any, s_any, sh_any, tf_any, after, out_any, token, x, s, sh, tf, mw, out, sems):
    @pl.when(info[COUNT] == 2)
    def _():
        for c in begin([(x_any.at[1], x), (s_any, s), (sh_any, sh), (tf_any, tf)], sems):
            c.wait()
        mask_taps(mw, tf, info[LBACK1] == 1, info[LBACK2] == 1)

        def body(t):
            at = pl.ds(t, MID)
            v = jnp.concatenate([flat(s[1, at]), flat(s[0, at]), flat(sh[at])], axis=-1)
            add_x(x, out, t, dot(v, mw[...]))

        steps(MID, body)

    @pl.when(info[COUNT] != 2)
    def _():
        out[...] = jnp.zeros_like(out)

    pltpu.sync_copy(out, out_any.at[1])
    token[...] = jnp.zeros_like(token)


def early_in_kernel(info, x_any, g_any, high_in, low_in, wb_any, tb_any, after, out_any, token, x, g, gn, wb, tb, mw, wide, out, sems):
    two = info[COUNT] == 2

    @pl.when(two)
    def _():
        need_n = begin_either(info[EVEN] == 1, low_in, high_in, gn, sems.at[4])
        for c in begin([(tb_any, tb), (g_any, g), (x_any.at[0], x), (wb_any, wb)], sems.at[pl.ds(0, 4)]) + [need_n]:
            c.wait()
        mask_taps(mw, tb, info[NEXT1] == 1, info[NEXT2] == 1)

        def upstream(t, n):
            at = pl.ds(t, n)
            return dot(jnp.concatenate([pair(g[0, at]), pair(g[1, at]), pair(gn[at])], axis=-1), mw[...])

        input_rows(wide, wb, upstream, x, g.at[0], out, 0, PAIRS)
        pltpu.sync_copy(out, out_any.at[0])

    @pl.when(jnp.logical_not(two))
    def _():
        out[...] = jnp.zeros_like(out)
        pltpu.sync_copy(out, out_any.at[1])
    token[...] = jnp.zeros_like(token)


def second_kernel(info, high_in, low_in, wf_any, out_ref, wide, xh, wf, sems):
    need_x = begin_either(info[EVEN] == 1, high_in, low_in, xh, sems.at[0])
    need_w = begin([(wf_any, wf)], sems.at[pl.ds(1, 1)])[0]
    clear_edges(wide)
    need_x.wait()
    fill_act(wide, lambda t, half: xh[pl.ds(t, FILL), half])
    need_w.wait()
    conv_to(out_ref, wide, wf)


def output_kernel(info, x_any, s_any, sh_any, s2_any, tf_any, early, out_any, token, x, s, sh, s2, tf, mw, out, sems):
    for c in begin([(x_any.at[0], x), (s_any.at[0], s), (sh_any, sh), (s2_any, s2), (tf_any, tf)], sems):
        c.wait()
    mask_taps(mw, tf, info[BACK1] == 1, info[BACK2] == 1)

    def body(t):
        at = pl.ds(t, MID)
        v = jnp.concatenate([flat(s[at]), flat(sh[at]), flat(s2[at])], axis=-1)
        add_x(x, out, t, dot(v, mw[...]))

    steps(MID, body)
    pltpu.sync_copy(out, out_any.at[0])
    token[...] = jnp.zeros_like(token)


def input_kernel(
    info, x_any, g_any, high1, low1, high2, low2, wb_any, tb_any, early, out_any, token,
    x, g, gn, gnn, wb, tb, mw, wide, out, sems, *, first
):
    two = info[COUNT] == 2
    even = info[EVEN] == 1
    last = jnp.where(two, 1, 0)
    need_n = begin_either(even, low1, high1, gn, sems.at[4])
    need_nn = begin_either(even, low2, high2, gnn, sems.at[5])
    need = begin([(tb_any, tb), (g_any.at[last], g), (wb_any, wb), (x_any.at[last], x)], sems.at[pl.ds(0, 4)])
    for c in need + [need_n, need_nn]:
        c.wait()
    mask_taps(
        mw, tb,
        jnp.where(two, info[LNEXT1], info[NEXT1]) == 1,
        jnp.where(two, info[LNEXT2], info[NEXT2]) == 1,
    )

    def upstream(t, n):
        at = pl.ds(t, n)
        return dot(jnp.concatenate([pair(g[at]), pair(gn[at]), pair(gnn[at])], axis=-1), mw[...])

    input_rows(wide, wb, upstream, x, g, out, first, PAIRS // 2)
    rows = pl.ds(first, PAIRS // 2)
    pltpu.sync_copy(out.at[rows], out_any.at[last, rows])
    token[...] = jnp.zeros_like(token)


def place_kernel(info, mine, theirs, spatial, temporal_out):
    at_x, at_y, core = info[AT_X], info[AT_Y], info[CORE]
    for half in range(2):
        for i in range(SIDE):
            for j in range(SIDE):
                a = lax.rem(at_x + SIDE - i, SIDE)
                b = lax.rem(at_y + SIDE - j, SIDE)
                piece = jnp.where(core == half, mine[a, b], theirs[a, b])
                row = half * HALF + (i * SIDE + j) * PIECE
                if row < 9 * CH:
                    spatial[row : row + PIECE] = piece
                else:
                    temporal_out[row - 9 * CH : row - 9 * CH + PIECE] = piece


FRAME = (PAIRS, 2, COLS, CH)
S_SHAPE = (PAIRS, COLS, 2 * CH)
WIDE = pltpu.VMEM((PAIRS + 1, COLS, 6 * CH), BF16)
VALUES = pltpu.VMEM(S_SHAPE, BF16)
W_SHAPE = (12 * CH, 2 * CH)
T_SHAPE = (6 * CH, 2 * CH)
TAPS = pltpu.VMEM(T_SHAPE, BF16)
TAPS2 = pltpu.VMEM((4 * CH, 2 * CH), BF16)
ACC = (2 * CH, 12 * CH)
TACC = (CH, 3 * CH)
PIECES = (SIDE, SIDE, PIECE, CH)
SMEM = pl.BlockSpec(memory_space=pltpu.SMEM)
VMEM = pl.BlockSpec(memory_space=pltpu.VMEM)
ANY = pl.BlockSpec(memory_space=pl.ANY)
HBM = pl.BlockSpec(memory_space=pltpu.HBM)
FRAME1 = pltpu.VMEM(FRAME, BF16)
FRAME2 = pltpu.VMEM((2,) + FRAME, BF16)
VALUES2 = pltpu.VMEM((2,) + S_SHAPE, BF16)
TAP = pltpu.VMEM((2 * CH, 2 * CH), BF16)
WEIGHT = pltpu.VMEM(W_SHAPE, BF16)


def shape(s, d=BF16):
    return jax.ShapeDtypeStruct(s, d)


def in_hbm(value):
    return pltpu.with_memory_space_constraint(value, pltpu.HBM)


def sems(n):
    return pltpu.SemaphoreType.DMA((n,))


def call(kernel, in_specs, outs, scratch, name, out_specs=None, aliases=None):
    return pl.pallas_call(
        kernel,
        in_specs=in_specs,
        out_specs=out_specs or [VMEM] * len(outs),
        out_shape=outs,
        scratch_shapes=scratch,
        input_output_aliases=aliases or {},
        compiler_params=pltpu.CompilerParams(vmem_limit_bytes=VMEM_BYTES),
        cost_estimate=pl.CostEstimate(flops=1, transcendentals=0, bytes_accessed=1),
        name=name,
    )


def shifts(value, axis, k):
    return lax.ppermute(value, axis, [(i, (i + k) % SIDE) for i in range(SIDE)])


def to_sum(parts, axis):
    return [parts[0]] + [shifts(parts[k], axis, k) for k in range(1, SIDE)]


def gather(part, axis):
    return [part] + [shifts(part, axis, k) for k in range(1, SIDE)]


def split_call(name, n_sum, n_out, out, n_after=0):
    def kernel(*refs):
        ins, outs = refs[:n_sum], refs[n_sum + n_after :]
        for n, out_ref in enumerate(outs):
            v = [r[n] if n_out > 1 else r[...] for r in ins]
            out_ref[...] = v[0] + v[1] if n_sum == 2 else (v[0] + v[2]) + (v[1] + v[3])

    return call(kernel, [VMEM] * n_sum + [ANY] * n_after, [shape(out, F32)] * n_out, [], name)


def stack_call(name, out, n_after):
    def kernel(*refs):
        for n in range(SIDE):
            refs[-1][n] = refs[n][...]

    run = call(kernel, [VMEM] * SIDE + [ANY] * n_after, [shape(out, F32)], [], name)
    return lambda *a: run(*a)[0]


def local(latents, cotangent, frame_counts, spatial_weight, temporal_weight):
    axes = ("x", "y", "z")
    here = lax.axis_index(axes)
    place = jnp.stack([here, lax.axis_index("dp")]).astype(jnp.int32)
    x = in_hbm(latents.reshape((2,) + FRAME))
    g = in_hbm(cotangent.reshape((2,) + FRAME))
    lows = range(0, N_SP, 2)
    low = [(i, i + 1) for i in lows] + [(i + 1, i) for i in lows]
    high = [(i + 1, (i + 2) % N_SP) for i in lows] + [((i + 2) % N_SP, i + 1) for i in lows]
    swap = [(0, 1), (1, 0)]

    info, for_high, for_low = call(
        prep_kernel,
        [SMEM, SMEM, HBM, HBM],
        [shape((INFO,), jnp.int32), shape(FRAME), shape(FRAME)],
        [sems(2)],
        "prep",
        [SMEM, ANY, ANY],
    )(frame_counts, place, x, g)
    high1 = lax.ppermute(for_high, axes, high)
    low1 = lax.ppermute(for_low, axes, low)

    s, acc, tacc, wf, wb, tf, tb = call(
        forward_kernel,
        [SMEM] + [HBM] * 4,
        [shape((2,) + S_SHAPE), shape(ACC, F32), shape(TACC, F32), shape(W_SHAPE), shape(W_SHAPE), shape(T_SHAPE), shape(T_SHAPE)],
        [
            WIDE, VALUES, TAPS2, FRAME2, FRAME2,
            pltpu.VMEM((3, 3, CH, CH), BF16), pltpu.VMEM((3, CH, CH), BF16), sems(4),
        ],
        "forward",
    )(info, x, g, spatial_weight, temporal_weight)

    info2, for_high, for_low = call(
        prep2_kernel,
        [SMEM] + [ANY] * 5,
        [shape((INFO,), jnp.int32), shape(FRAME), shape(FRAME)],
        [sems(2)],
        "prep2",
        [SMEM, ANY, ANY],
    )(info, x, g, high1, low1, tacc)
    high2 = lax.ppermute(for_high, axes, high)
    low2 = lax.ppermute(for_low, axes, low)

    own, other, sh = call(
        grad_kernel,
        [SMEM] + [ANY] * 9,
        [shape(PIECES, F32), shape(PIECES, F32), shape(S_SHAPE)],
        [
            WIDE, FRAME1, FRAME1, FRAME1, FRAME2, VALUES, VALUES, VALUES,
            pltpu.VMEM(ACC, F32), pltpu.VMEM(TACC, F32), WEIGHT, TAPS, TAPS2, pltpu.VMEM((2, HALF, CH), F32), sems(10),
        ],
        "grads",
        [VMEM, VMEM, ANY],
    )(info2, high1, low1, x, g, s, acc, tacc, wf, tb)

    chunks = split_call("core_sum", 2, SIDE, PIECES[1:])(own, lax.ppermute(other, "dp", swap))
    frames = [pltpu.HBM((2,) + FRAME, BF16), shape((8, CH), F32)]
    early_out, done_a = call(
        early_out_kernel,
        [SMEM] + [ANY] * 5,
        frames,
        [FRAME1, VALUES2, VALUES, TAPS, TAPS, FRAME1, sems(4)],
        "early_out",
        [ANY, VMEM],
    )(info, x, s, sh, tf, chunks[0])
    early_in, done_b = call(
        early_in_kernel,
        [SMEM] + [ANY] * 7,
        frames,
        [FRAME1, FRAME2, FRAME1, WEIGHT, TAPS, TAPS, WIDE, FRAME1, sems(5)],
        "early_in",
        [ANY, VMEM],
    )(info, x, g, high1, low1, wb, tb, chunks[0])
    chunks = split_call("x_sum", SIDE, SIDE, PIECES[2:], 2)(*to_sum(chunks, "x"), done_a, done_b)
    s2 = call(second_kernel, [SMEM] + [ANY] * 3, [shape(S_SHAPE)], [WIDE, FRAME1, WEIGHT, sems(2)], "second")(info, high2, low2, wf)[0]
    part = split_call("y_sum", SIDE, 1, PIECES[2:], 1)(*to_sum(chunks, "y"), s2)[0]
    block_out, done_c = call(
        output_kernel,
        [SMEM] + [ANY] * 6,
        frames,
        [FRAME1, VALUES, VALUES, VALUES, TAPS, TAPS, FRAME1, sems(5)],
        "output",
        [ANY, VMEM],
        {6: 0},
    )(info, x, s, sh, s2, tf, in_hbm(early_out))
    part = split_call("z_sum", SIDE, 1, PIECES[2:], 1)(*to_sum([part] * SIDE, "z"), done_c)[0]

    def input_half(first, so_far):
        return call(
            functools.partial(input_kernel, first=first),
            [SMEM] + [ANY] * 9,
            frames,
            [FRAME1, FRAME1, FRAME1, FRAME1, WEIGHT, TAPS, TAPS, WIDE, FRAME1, sems(6)],
            "input_grad",
            [ANY, VMEM],
            {9: 0},
        )(info, x, g, high1, low1, high2, low2, wb, tb, in_hbm(so_far))

    input_grad, done_d = input_half(0, early_in)
    own = stack_call("y_stack", PIECES[1:], 1)(*gather(part, "y"), done_d)
    input_grad, done_e = input_half(PAIRS // 2, input_grad)
    own = stack_call("x_stack", PIECES, 1)(*gather(own, "x"), done_e)
    theirs = lax.ppermute(own, "dp", swap)
    spatial_grad, temporal_grad = call(
        place_kernel, [SMEM, VMEM, VMEM], [shape((9 * CH, CH), F32), shape((3 * CH, CH), F32)], [], "place"
    )(info, own, theirs)
    return (
        block_out.reshape(latents.shape),
        input_grad.reshape(latents.shape),
        spatial_grad.reshape(3, 3, CH, CH),
        temporal_grad.reshape(3, CH, CH),
    )


def solution(mesh):
    chips = Mesh(mesh.devices.reshape(2, SIDE, SIDE, SIDE), ("dp", "x", "y", "z"))
    held = P(("dp", "x", "y", "z"), None, None, None)
    return jax.shard_map(
        local,
        mesh=chips,
        in_specs=(held, held, P("dp", None), P(), P()),
        out_specs=(held, held, P(), P()),
        check_vma=False,
    )
```

```python
import functools

import jax
import jax.numpy as jnp
from jax import lax
from jax.experimental import pallas as pl
from jax.experimental.pallas import tpu as pltpu
from jax.sharding import Mesh
from jax.sharding import PartitionSpec as P

FRAMES = 9
CLIPS = 8
CH = 128
ROWS = 64
COLS = 64
N_SP = 64
SIDE = 4
PAIRS = ROWS // 2
F32 = jnp.float32
BF16 = jnp.bfloat16
VMEM_BYTES = 24 * 1024 * 1024
SCALE = float(2 * CLIPS * FRAMES * ROWS * COLS) ** (-0.5)
HALF = 6 * CH
PIECE = HALF // SIDE

COUNT, EVEN, BACK1, NEXT1, NEXT2, LBACK1, LBACK2, LNEXT1, CORE, AT_X = range(10)
INFO = (8, 128)

FILL = 8
MID = 16
FULL = 32


def dot(a, b):
    return jnp.dot(a, b, preferred_element_type=F32)


def dot_t(a, b):
    return lax.dot_general(a, b, (((0,), (0,)), ((), ())), preferred_element_type=F32)


def steps(block, body):
    def one(n, _):
        body(n * block)
        return 0

    lax.fori_loop(0, PAIRS // block, one, 0)


def clear_edges(wide):
    wide[0, :, 0 : 3 * CH] = jnp.zeros((COLS, 3 * CH), BF16)
    wide[PAIRS, :, 3 * CH : 6 * CH] = jnp.zeros((COLS, 3 * CH), BF16)


def put_row(wide, t, half, a):
    col = lax.broadcasted_iota(jnp.int32, a.shape, 1)
    before = jnp.where(col == 0, 0.0, pltpu.roll(a, 1, 1))
    after = jnp.where(col == COLS - 1, 0.0, pltpu.roll(a, COLS - 1, 1))
    at = pl.ds(t + half, a.shape[0])
    base = 0 if half else 3 * CH
    wide[at, :, base : base + CH] = before.astype(BF16)
    wide[at, :, base + CH : base + 2 * CH] = a.astype(BF16)
    wide[at, :, base + 2 * CH : base + 3 * CH] = after.astype(BF16)


def fill_act(wide, rows):
    def body(t):
        for half in range(2):
            x = rows(t, half).astype(F32)
            put_row(wide, t, half, x * jax.nn.sigmoid(x))

    steps(FILL, body)


def windows(wide, t, block):
    low = wide[pl.ds(t, block)].reshape(block * COLS, 6 * CH)
    high = wide[pl.ds(t + 1, block)].reshape(block * COLS, 6 * CH)
    return low, high


def conv(wide, w_ref, t, block):
    low, high = windows(wide, t, block)
    return dot(low, w_ref[0 : 6 * CH, :]) + dot(high, w_ref[6 * CH : 12 * CH, :])


def conv_to(out_ref, wide, w_ref):
    def body(t):
        out_ref[pl.ds(t, FULL)] = conv(wide, w_ref, t, FULL).astype(BF16).reshape(FULL, COLS, 2 * CH)

    steps(FULL, body)


def pair(v):
    return jnp.concatenate([v[:, 0], v[:, 1]], axis=-1).reshape(v.shape[0] * COLS, 2 * CH)


def flat(v):
    return v.reshape(v.shape[0] * COLS, 2 * CH)


def add_spatial(acc, wide, v_ref):
    def body(t):
        low, high = windows(wide, t, FULL)
        v = flat(v_ref[pl.ds(t, FULL)])
        acc[:, 0 : 6 * CH] += dot_t(v, low)
        acc[:, 6 * CH : 12 * CH] += dot_t(v, high)

    steps(FULL, body)


def correlate(s, gs):
    total = None
    for half in range(2):
        a = s[:, :, half * CH : half * CH + CH].reshape(PAIRS * COLS, CH)
        b = gs(half)
        one = dot_t(a, b.reshape(PAIRS * COLS, b.shape[-1]))
        total = one if total is None else total + one
    return total


def copy_either(first, a, b, sem):
    @pl.when(first)
    def _():
        pltpu.make_async_copy(*a, sem).start()

    @pl.when(jnp.logical_not(first))
    def _():
        pltpu.make_async_copy(*b, sem).start()

    return pltpu.make_async_copy(*a, sem)


def is_two(info):
    return info[0, COUNT] == 2


def is_set(info, n):
    return info[0, n] == 1


def either(first, a, b):
    return lambda *at: jnp.where(first, a[at], b[at])


def prep_kernel(counts, x_hbm, g_hbm, info, high_ref, low_ref, sems):
    here = (lax.axis_index("x") * SIDE + lax.axis_index("y")) * SIDE + lax.axis_index("z")
    even = here % 2 == 0

    def put(source, for_high, sem):
        return copy_either(for_high, (source, high_ref), (source, low_ref), sem)

    down = put(g_hbm.at[0], even, sems.at[0])
    c = counts[...].astype(F32)
    order = lax.broadcasted_iota(jnp.int32, c.shape, 1)
    start = jnp.sum(jnp.where(order < here, c, 0.0)).astype(jnp.int32)
    count = jnp.sum(jnp.where(order == here, c, 0.0)).astype(jnp.int32)
    up = put(x_hbm.at[jnp.where(count == 2, 1, 0)], jnp.logical_not(even), sems.at[1])
    first = start % FRAMES
    second = (first + 1) % FRAMES
    final = FRAMES - 1
    values = {
        COUNT: count,
        EVEN: even.astype(jnp.int32),
        BACK1: (first >= 1).astype(jnp.int32),
        NEXT1: (first + 1 <= final).astype(jnp.int32),
        NEXT2: (first + 2 <= final).astype(jnp.int32),
        LBACK1: (second >= 1).astype(jnp.int32),
        LBACK2: (second >= 2).astype(jnp.int32),
        LNEXT1: (second + 1 <= final).astype(jnp.int32),
        CORE: lax.axis_index("dp"),
        AT_X: lax.axis_index("x"),
    }
    lane = lax.broadcasted_iota(jnp.int32, INFO, 1)
    found = jnp.zeros(INFO, jnp.int32)
    for n, value in values.items():
        found = jnp.where(lane == n, value, found)
    info[...] = found
    down.wait()
    up.wait()


def forward_kernel(info, x_ref, g_ref, w_ref, tw_ref, s_ref, acc, tacc, wf, wb, tf, tb, wide, v_ref, mw):
    zero = jnp.zeros((CH, CH), BF16)
    for a in range(4):
        for q in range(3):
            rows = slice((a * 3 + q) * CH, (a * 3 + q + 1) * CH)
            for b in range(2):
                lanes = slice(b * CH, b * CH + CH)
                inside = 0 <= a - b <= 2
                wf[rows, lanes] = w_ref[a - b, q] if inside else zero
                wb[rows, lanes] = w_ref[2 - (a - b), 2 - q].T if inside else zero
    for k in range(3):
        for a in range(2):
            rows = slice((2 * k + a) * CH, (2 * k + a + 1) * CH)
            for b in range(2):
                lanes = slice(b * CH, b * CH + CH)
                tf[rows, lanes] = tw_ref[k] if a == b else zero
                tb[rows, lanes] = tw_ref[k].T if a == b else zero

    acc[...] = jnp.zeros_like(acc)
    tacc[...] = jnp.zeros_like(tacc)
    clear_edges(wide)
    mw[0 : 2 * CH] = tb[0 : 2 * CH]

    def slot(j, _):
        keep = jnp.logical_and(j == 0, jnp.logical_and(is_two(info), is_set(info, NEXT1)))
        mw[2 * CH : 4 * CH] = jnp.where(keep, tb[2 * CH : 4 * CH], jnp.zeros((2 * CH, 2 * CH), BF16))
        fill_act(wide, lambda t, half: x_ref[j, pl.ds(t, FILL), half])
        conv_to(s_ref.at[j], wide, wf)

        def upstream(t):
            at = pl.ds(t, MID)
            both = jnp.concatenate([pair(g_ref[j, at]), pair(g_ref[1, at])], axis=-1)
            v_ref[at] = dot(both, mw[...]).astype(BF16).reshape(MID, COLS, 2 * CH)

        steps(MID, upstream)
        add_spatial(acc, wide, v_ref)
        found = correlate(s_ref[j], lambda half: jnp.concatenate([g_ref[j, :, half], g_ref[1, :, half]], axis=-1))
        tacc[:, 0:CH] += found[:, 0:CH]
        tacc[:, CH : 2 * CH] += jnp.where(keep, found[:, CH : 2 * CH], 0.0)
        return 0

    lax.fori_loop(0, info[0, COUNT], slot, 0)


def mid_kernel(info, high_in, low_in, s, g, wf, tf, tb, sent, sh, wide, mw):
    two = is_two(info)
    even = is_set(info, EVEN)
    back = is_set(info, BACK1)
    before, after = either(even, high_in, low_in), either(even, low_in, high_in)
    clear_edges(wide)
    fill_act(wide, lambda t, half: before(pl.ds(t, FILL), half))
    conv_to(sh, wide, wf)

    down = jnp.where(even, 0, 1)
    nothing = jnp.zeros((2 * CH, 2 * CH), BF16)
    mw[0 : 2 * CH] = jnp.where(back, tb[2 * CH : 4 * CH], nothing)
    mw[2 * CH : 4 * CH] = jnp.where(jnp.logical_and(back, is_set(info, NEXT1)), tb[4 * CH : 6 * CH], nothing)

    def upstream(t):
        at = pl.ds(t, FULL)
        v = jnp.concatenate([pair(g[0, at]), pair(jnp.where(two, g[1, at], after(at)))], axis=-1)
        sent[down, at] = dot(v, mw[...]).astype(BF16).reshape(FULL, COLS, 2 * CH)

    steps(FULL, upstream)
    keep1 = jnp.where(two, info[0, LNEXT1], info[0, NEXT1]) == 1
    keep2 = jnp.logical_and(keep1, jnp.where(two, info[0, LBACK1], info[0, BACK1]) == 1)
    mw[0 : 2 * CH] = jnp.where(keep1, tf[2 * CH : 4 * CH], nothing)
    mw[2 * CH : 4 * CH] = jnp.where(keep2, tf[4 * CH : 6 * CH], nothing)

    def ahead(t):
        at = pl.ds(t, FULL)
        v = jnp.concatenate([flat(jnp.where(two, s[1, at], s[0, at])), flat(jnp.where(two, s[0, at], sh[at]))], axis=-1)
        sent[1 - down, at] = dot(v, mw[...]).astype(BF16).reshape(FULL, COLS, 2 * CH)

    steps(FULL, ahead)


def grad_kernel(info, high_in, low_in, x, g, s, sent, sh, acc_in, tacc_in, tb, own_ref, other_ref, wide, v, acc, tacc, both):
    two = is_two(info)
    even = is_set(info, EVEN)
    back = is_set(info, BACK1)
    cross = jnp.logical_and(back, is_set(info, NEXT1))
    before, after = either(even, high_in, low_in), either(even, low_in, high_in)
    down = jnp.where(even, 0, 1)
    acc[...] = acc_in[...]
    tacc[...] = tacc_in[...]
    clear_edges(wide)
    fill_act(wide, lambda t, half: before(pl.ds(t, FILL), half))
    add_spatial(acc, wide, sent.at[down])
    rows = slice(None)

    def two_frames(half):
        return jnp.concatenate([g[0, :, half], jnp.where(two, g[1, :, half], after(rows, half))], axis=-1)

    found = correlate(sh[...], two_frames)
    tacc[:, CH : 2 * CH] += jnp.where(back, found[:, 0:CH], 0.0)
    tacc[:, 2 * CH : 3 * CH] += jnp.where(cross, found[:, CH : 2 * CH], 0.0)

    @pl.when(jnp.logical_and(two, is_set(info, NEXT2)))
    def _():
        fill_act(wide, lambda t, half: x[0, pl.ds(t, FILL), half])

        def up(t):
            at = pl.ds(t, MID)
            v[at] = dot(pair(after(at)), tb[4 * CH : 6 * CH]).astype(BF16).reshape(MID, COLS, 2 * CH)

        steps(MID, up)
        add_spatial(acc, wide, v)
        tacc[:, 2 * CH : 3 * CH] += correlate(s[0], lambda half: after(rows, half))

    at_x, core = info[0, AT_X], info[0, CORE]
    for p in range(3):
        for q in range(3):
            first = (p * 3 + q) * CH
            second = ((p + 1) * 3 + q) * CH
            found = acc[0:CH, first : first + CH] + acc[CH : 2 * CH, second : second + CH]
            n = p * 3 + q
            both[n // 6, (n % 6) * CH : (n % 6 + 1) * CH] = found.T * SCALE
    for k in range(3):
        both[1, (3 + k) * CH : (4 + k) * CH] = tacc[:, k * CH : k * CH + CH] * SCALE
    for i in range(SIDE):
        source = pl.ds(pl.multiple_of(lax.rem(at_x + i, SIDE) * PIECE, PIECE), PIECE)
        own_ref[i] = both[core, source]
        other_ref[i] = both[1 - core, source]


def add_x(x, slot, out, to, sem, t, value):
    at = pl.ds(t, MID)
    value = value.astype(BF16).astype(F32).reshape(MID, COLS, 2 * CH)
    for half in range(2):
        out[at, half] = (x[slot, at, half].astype(F32) + value[:, :, half * CH : half * CH + CH]).astype(BF16)
    pltpu.make_async_copy(out.at[at], to.at[at], sem).start()


def mask_taps(mw, taps, keep1, keep2):
    nothing = jnp.zeros((2 * CH, 2 * CH), BF16)
    mw[0 : 2 * CH] = taps[0 : 2 * CH]
    mw[2 * CH : 4 * CH] = jnp.where(keep1, taps[2 * CH : 4 * CH], nothing)
    mw[4 * CH : 6 * CH] = jnp.where(keep2, taps[4 * CH : 6 * CH], nothing)


def input_rows(wide, wb, upstream, x, g, slot, out, to, sem, first, count):
    clear_edges(wide)

    def up(t, n):
        value = upstream(t, n).reshape(n, COLS, 2 * CH)
        for half in range(2):
            put_row(wide, t, half, value[:, :, half * CH : half * CH + CH])

    def up_full(n, _):
        up(first + n * FILL, FILL)
        return 0

    lax.fori_loop(0, count // FILL, up_full, 0)
    if first > 0:
        up(first - 1, 1)
    if first + count < PAIRS:
        up(first + count, 1)

    def down(n, _):
        t = first + n * MID
        at = pl.ds(t, MID)
        back = conv(wide, wb, t, MID).reshape(MID, COLS, 2 * CH)
        for half in range(2):
            xv = x[slot, at, half].astype(F32)
            sig = jax.nn.sigmoid(xv)
            b = back[:, :, half * CH : half * CH + CH]
            out[at, half] = (g[slot, at, half].astype(F32) + b * (sig * (1.0 + xv * (1.0 - sig)))).astype(BF16)
        pltpu.make_async_copy(out.at[at], to.at[at], sem).start()
        return 0

    lax.fori_loop(0, count // MID, down, 0)


def early_out_kernel(info, x, s, sh, tf, after, out_any, token, mw, out, sem):
    to = out_any.at[1]

    @pl.when(is_two(info))
    def _():
        mask_taps(mw, tf, is_set(info, LBACK1), is_set(info, LBACK2))

        def body(t):
            at = pl.ds(t, MID)
            v = jnp.concatenate([flat(s[1, at]), flat(s[0, at]), flat(sh[at])], axis=-1)
            add_x(x, 1, out, to, sem, t, dot(v, mw[...]))

        steps(MID, body)

    @pl.when(jnp.logical_not(is_two(info)))
    def _():
        out[...] = jnp.zeros_like(out)
        pltpu.make_async_copy(out, to, sem).start()

    token[...] = jnp.zeros_like(token)
    pltpu.make_async_copy(out, to, sem).wait()


def early_in_kernel(info, x, g, high_in, low_in, wb, tb, after, out_any, token, mw, wide, out, sem):
    two = is_two(info)
    coming = either(is_set(info, EVEN), low_in, high_in)

    @pl.when(two)
    def _():
        mask_taps(mw, tb, is_set(info, NEXT1), is_set(info, NEXT2))

        def upstream(t, n):
            at = pl.ds(t, n)
            return dot(jnp.concatenate([pair(g[0, at]), pair(g[1, at]), pair(coming(at))], axis=-1), mw[...])

        input_rows(wide, wb, upstream, x, g, 0, out, out_any.at[0], sem, 0, PAIRS)

    @pl.when(jnp.logical_not(two))
    def _():
        out[...] = jnp.zeros_like(out)
        pltpu.make_async_copy(out, out_any.at[1], sem).start()

    token[...] = jnp.zeros_like(token)
    pltpu.make_async_copy(out, out_any.at[1], sem).wait()


def output_kernel(info, x, s, high_in, low_in, tf, early, out_any, token, out, sem):
    ahead = either(is_set(info, EVEN), high_in, low_in)
    to = out_any.at[0]

    def body(t):
        at = pl.ds(t, MID)
        add_x(x, 0, out, to, sem, t, dot(flat(s[0, at]), tf[0 : 2 * CH]) + flat(ahead(at)).astype(F32))

    steps(MID, body)
    token[...] = jnp.zeros_like(token)
    pltpu.make_async_copy(out, to, sem).wait()


def input_kernel(info, x, g, high_in, low_in, wb, tb, early, out_any, token, wide, out, sem, *, first):
    last = jnp.where(is_two(info), 1, 0)
    share = either(is_set(info, EVEN), low_in, high_in)
    to = out_any.at[last]

    def upstream(t, n):
        at = pl.ds(t, n)
        return dot(pair(g[last, at]), tb[0 : 2 * CH]) + flat(share(at)).astype(F32)

    input_rows(wide, wb, upstream, x, g, last, out, to, sem, first, PAIRS // 2)
    token[...] = jnp.zeros_like(token)
    rows = pl.ds(first, PAIRS // 2)
    pltpu.make_async_copy(out.at[rows], to.at[rows], sem).wait()


def place_kernel(info, mine, theirs, spatial, temporal_out):
    at_x, core = info[0, AT_X], info[0, CORE]
    for half in range(2):
        for i in range(SIDE):
            n = lax.rem(at_x + SIDE - i, SIDE)
            piece = jnp.where(core == half, mine[n], theirs[n])
            row = half * HALF + i * PIECE
            if row < 9 * CH:
                spatial[row : row + PIECE] = piece
            else:
                temporal_out[row - 9 * CH : row - 9 * CH + PIECE] = piece


FRAME = (PAIRS, 2, COLS, CH)
S_SHAPE = (PAIRS, COLS, 2 * CH)
WIDE = pltpu.VMEM((PAIRS + 1, COLS, 6 * CH), BF16)
VALUES = pltpu.VMEM(S_SHAPE, BF16)
W_SHAPE = (12 * CH, 2 * CH)
T_SHAPE = (6 * CH, 2 * CH)
TAPS = pltpu.VMEM(T_SHAPE, BF16)
TAPS2 = pltpu.VMEM((4 * CH, 2 * CH), BF16)
ACC = (2 * CH, 12 * CH)
TACC = (CH, 3 * CH)
PIECES = (SIDE, PIECE, CH)
VMEM = pl.BlockSpec(memory_space=pltpu.VMEM)
ANY = pl.BlockSpec(memory_space=pl.ANY)
HBM = pl.BlockSpec(memory_space=pltpu.HBM)
FRAME1 = pltpu.VMEM(FRAME, BF16)
SEM = pltpu.SemaphoreType.DMA
def shape(s, d=BF16):
    return jax.ShapeDtypeStruct(s, d)


def in_hbm(value):
    return pltpu.with_memory_space_constraint(value, pltpu.HBM)


def call(kernel, in_specs, outs, scratch, name, out_specs=None, aliases=None):
    return pl.pallas_call(
        kernel,
        in_specs=in_specs,
        out_specs=out_specs or [VMEM] * len(outs),
        out_shape=outs,
        scratch_shapes=scratch,
        input_output_aliases=aliases or {},
        compiler_params=pltpu.CompilerParams(vmem_limit_bytes=VMEM_BYTES),
        cost_estimate=pl.CostEstimate(flops=1, transcendentals=0, bytes_accessed=1),
        name=name,
    )


def shifts(value, axis, k):
    return lax.ppermute(value, axis, [(i, (i + k) % SIDE) for i in range(SIDE)])


def to_sum(parts, axis):
    return [parts[0]] + [shifts(parts[k], axis, k) for k in range(1, SIDE)]


def gather(part, axis):
    return [part] + [shifts(part, axis, k) for k in range(1, SIDE)]


def split_call(name, n_sum, n_out, out, n_after=0):
    def kernel(*refs):
        ins, outs = refs[:n_sum], refs[n_sum + n_after :]
        for n, out_ref in enumerate(outs):
            v = [r[n] if n_out > 1 else r[...] for r in ins]
            out_ref[...] = v[0] + v[1] if n_sum == 2 else (v[0] + v[2]) + (v[1] + v[3])

    return call(kernel, [VMEM] * n_sum + [ANY] * n_after, [shape(out, F32)] * n_out, [], name)


def stack_call(name, out, n_after):
    def kernel(*refs):
        for n in range(SIDE):
            refs[-1][n] = refs[n][...]

    run = call(kernel, [VMEM] * SIDE + [ANY] * n_after, [shape(out, F32)], [], name)
    return lambda *a: run(*a)[0]


def local(latents, cotangent, frame_counts, spatial_weight, temporal_weight):
    axes = ("x", "y", "z")
    x = latents.reshape((2,) + FRAME)
    g = cotangent.reshape((2,) + FRAME)
    lows = range(0, N_SP, 2)
    low = [(i, i + 1) for i in lows] + [(i + 1, i) for i in lows]
    high = [(i + 1, (i + 2) % N_SP) for i in lows] + [((i + 2) % N_SP, i + 1) for i in lows]
    swap = [(0, 1), (1, 0)]

    info, for_high, for_low = call(
        prep_kernel,
        [VMEM, HBM, HBM],
        [shape(INFO, jnp.int32), shape(FRAME), shape(FRAME)],
        [SEM((2,))],
        "prep",
        [VMEM, ANY, ANY],
    )(frame_counts, in_hbm(x), in_hbm(g))
    high1 = lax.ppermute(for_high, axes, high)
    low1 = lax.ppermute(for_low, axes, low)

    s, acc, tacc, wf, wb, tf, tb = call(
        forward_kernel,
        [VMEM] * 5,
        [shape((2,) + S_SHAPE), shape(ACC, F32), shape(TACC, F32), shape(W_SHAPE), shape(W_SHAPE), shape(T_SHAPE), shape(T_SHAPE)],
        [WIDE, VALUES, TAPS2],
        "forward",
    )(info, x, g, spatial_weight, temporal_weight)

    sent, sh = call(
        mid_kernel, [VMEM] * 8, [shape((2,) + S_SHAPE), shape(S_SHAPE)], [WIDE, TAPS2], "mid"
    )(info, high1, low1, s, g, wf, tf, tb)
    high2 = lax.ppermute(sent[0], axes, high)
    low2 = lax.ppermute(sent[1], axes, low)

    own, other = call(
        grad_kernel,
        [VMEM] * 11,
        [shape(PIECES, F32), shape(PIECES, F32)],
        [WIDE, VALUES, pltpu.VMEM(ACC, F32), pltpu.VMEM(TACC, F32), pltpu.VMEM((2, HALF, CH), F32)],
        "grads",
    )(info, high1, low1, x, g, s, sent, sh, acc, tacc, tb)

    chunks = split_call("core_sum", 2, SIDE, PIECES[1:])(own, lax.ppermute(other, "dp", swap))
    frames = [pltpu.HBM((2,) + FRAME, BF16), shape((8, CH), F32)]
    early_out, done_a = call(
        early_out_kernel, [VMEM] * 5 + [ANY], frames, [TAPS, FRAME1, SEM], "early_out", [ANY, VMEM]
    )(info, x, s, sh, tf, chunks[0])
    early_in, done_b = call(
        early_in_kernel, [VMEM] * 7 + [ANY], frames, [TAPS, WIDE, FRAME1, SEM], "early_in", [ANY, VMEM]
    )(info, x, g, high1, low1, wb, tb, chunks[0])
    part = split_call("x_sum", SIDE, 1, PIECES[1:], 2)(*to_sum(chunks, "x"), done_a, done_b)[0]
    block_out, done_c = call(
        output_kernel, [VMEM] * 6 + [ANY], frames, [FRAME1, SEM], "output", [ANY, VMEM], {6: 0}
    )(info, x, s, high2, low2, tf, in_hbm(early_out))
    part = split_call("y_sum", SIDE, 1, PIECES[1:], 1)(*gather(part, "y"), done_c)[0]

    def input_half(first, so_far):
        return call(
            functools.partial(input_kernel, first=first),
            [VMEM] * 7 + [ANY],
            frames,
            [WIDE, FRAME1, SEM],
            "input_grad",
            [ANY, VMEM],
            {7: 0},
        )(info, x, g, high2, low2, wb, tb, in_hbm(so_far))

    input_grad, done_d = input_half(0, early_in)
    part = split_call("z_sum", SIDE, 1, PIECES[1:], 1)(*gather(part, "z"), done_d)[0]
    input_grad, done_e = input_half(PAIRS // 2, input_grad)
    own = stack_call("x_stack", PIECES, 1)(*gather(part, "x"), done_e)
    theirs = lax.ppermute(own, "dp", swap)
    spatial_grad, temporal_grad = call(
        place_kernel, [VMEM, VMEM, VMEM], [shape((9 * CH, CH), F32), shape((3 * CH, CH), F32)], [], "place"
    )(info, own, theirs)
    return (
        block_out.reshape(latents.shape),
        input_grad.reshape(latents.shape),
        spatial_grad.reshape(3, 3, CH, CH),
        temporal_grad.reshape(3, CH, CH),
    )


def solution(mesh):
    chips = Mesh(mesh.devices.reshape(2, SIDE, SIDE, SIDE), ("dp", "x", "y", "z"))
    held = P(("dp", "x", "y", "z"), None, None, None)
    return jax.shard_map(
        local,
        mesh=chips,
        in_specs=(held, held, P("dp", None), P(), P()),
        out_specs=(held, held, P(), P()),
        check_vma=False,
    )
```

```python
import functools

import jax
import jax.numpy as jnp
from jax import lax
from jax.experimental import pallas as pl
from jax.experimental.pallas import tpu as pltpu
from jax.sharding import Mesh
from jax.sharding import PartitionSpec as P

FRAMES = 9
CLIPS = 8
CH = 128
ROWS = 64
COLS = 64
N_SP = 64
SIDE = 4
PAIRS = ROWS // 2
F32 = jnp.float32
BF16 = jnp.bfloat16
VMEM_BYTES = 24 * 1024 * 1024
SCALE = float(2 * CLIPS * FRAMES * ROWS * COLS) ** (-0.5)
HALF = 6 * CH
PIECE = HALF // SIDE

COUNT, EVEN, BACK1, NEXT1, NEXT2, LBACK1, LBACK2, LNEXT1, CORE, AT_X = range(10)
INFO = (8, 128)

FILL = 8
MID = 16
FULL = 32
CUT1 = 16
CUT2 = 15


def dot(a, b):
    return jnp.dot(a, b, preferred_element_type=F32)


def dot_t(a, b):
    return lax.dot_general(a, b, (((0,), (0,)), ((), ())), preferred_element_type=F32)


def steps(block, body):
    def one(n, _):
        body(n * block)
        return 0

    lax.fori_loop(0, PAIRS // block, one, 0)


def clear_edges(wide):
    wide[0, :, 0 : 3 * CH] = jnp.zeros((COLS, 3 * CH), BF16)
    wide[PAIRS, :, 3 * CH : 6 * CH] = jnp.zeros((COLS, 3 * CH), BF16)


def put_row(wide, t, half, a):
    col = lax.broadcasted_iota(jnp.int32, a.shape, 1)
    before = jnp.where(col == 0, 0.0, pltpu.roll(a, 1, 1))
    after = jnp.where(col == COLS - 1, 0.0, pltpu.roll(a, COLS - 1, 1))
    at = pl.ds(t + half, a.shape[0])
    base = 0 if half else 3 * CH
    wide[at, :, base : base + CH] = before.astype(BF16)
    wide[at, :, base + CH : base + 2 * CH] = a.astype(BF16)
    wide[at, :, base + 2 * CH : base + 3 * CH] = after.astype(BF16)


def put_act(wide, t, half, x):
    x = x.astype(F32)
    put_row(wide, t, half, x * jax.nn.sigmoid(x))


def fill_act(wide, rows, first=0, count=PAIRS):
    for t in range(first, first + count, FILL):
        for half in range(2):
            put_act(wide, t, half, rows(t, FILL, half))


def windows(wide, t, block):
    low = wide[pl.ds(t, block)].reshape(block * COLS, 6 * CH)
    high = wide[pl.ds(t + 1, block)].reshape(block * COLS, 6 * CH)
    return low, high


def conv(wide, w_ref, t, block):
    low, high = windows(wide, t, block)
    return dot(low, w_ref[0 : 6 * CH, :]) + dot(high, w_ref[6 * CH : 12 * CH, :])


def conv_to(out_ref, wide, w_ref):
    def body(t):
        out_ref[pl.ds(t, FULL)] = conv(wide, w_ref, t, FULL).astype(BF16).reshape(FULL, COLS, 2 * CH)

    steps(FULL, body)


def pair(v):
    return jnp.concatenate([v[:, 0], v[:, 1]], axis=-1).reshape(v.shape[0] * COLS, 2 * CH)


def flat(v):
    return v.reshape(v.shape[0] * COLS, 2 * CH)


def add_spatial(acc, wide, v_ref):
    def body(t):
        low, high = windows(wide, t, FULL)
        v = flat(v_ref[pl.ds(t, FULL)])
        acc[:, 0 : 6 * CH] += dot_t(v, low)
        acc[:, 6 * CH : 12 * CH] += dot_t(v, high)

    steps(FULL, body)


def correlate(s, gs):
    total = None
    for half in range(2):
        a = s[:, :, half * CH : half * CH + CH].reshape(s.shape[0] * COLS, CH)
        b = gs(half)
        one = dot_t(a, b.reshape(s.shape[0] * COLS, b.shape[-1]))
        total = one if total is None else total + one
    return total


def copy_either(first, a, b, sem):
    @pl.when(first)
    def _():
        pltpu.make_async_copy(*a, sem).start()

    @pl.when(jnp.logical_not(first))
    def _():
        pltpu.make_async_copy(*b, sem).start()

    return pltpu.make_async_copy(*a, sem)


def is_two(info):
    return info[0, COUNT] == 2


def is_set(info, n):
    return info[0, n] == 1


def either(first, a, b):
    return lambda *at: jnp.where(first, a[at], b[at])


def halves(first, a, b, cut):
    parts = (either(first, a[0], b[0]), either(first, a[1], b[1]))

    def read(t, n, *at):
        found = []
        if t < cut:
            found.append(parts[0](pl.ds(t, min(n, cut - t)), *at))
        if t + n > cut:
            start = max(t, cut)
            found.append(parts[1](pl.ds(start - cut, t + n - start), *at))
        return found[0] if len(found) == 1 else jnp.concatenate(found, axis=0)

    return read


def prep_kernel(counts, x_hbm, g_hbm, info, high_a, low_a, high_b, low_b, sems):
    here = (lax.axis_index("x") * SIDE + lax.axis_index("y")) * SIDE + lax.axis_index("z")
    even = here % 2 == 0

    top, bottom = pl.ds(0, CUT1), pl.ds(CUT1, PAIRS - CUT1)

    def put(source, slot, for_high, n):
        a = copy_either(for_high, (source.at[slot, top], high_a), (source.at[slot, top], low_a), sems.at[n])
        b = copy_either(for_high, (source.at[slot, bottom], high_b), (source.at[slot, bottom], low_b), sems.at[n + 1])
        return [a, b]

    copies = put(g_hbm, 0, even, 0)
    c = counts[...].astype(F32)
    order = lax.broadcasted_iota(jnp.int32, c.shape, 1)
    start = jnp.sum(jnp.where(order < here, c, 0.0)).astype(jnp.int32)
    count = jnp.sum(jnp.where(order == here, c, 0.0)).astype(jnp.int32)
    copies += put(x_hbm, jnp.where(count == 2, 1, 0), jnp.logical_not(even), 2)
    first = start % FRAMES
    second = (first + 1) % FRAMES
    final = FRAMES - 1
    values = {
        COUNT: count,
        EVEN: even.astype(jnp.int32),
        BACK1: (first >= 1).astype(jnp.int32),
        NEXT1: (first + 1 <= final).astype(jnp.int32),
        NEXT2: (first + 2 <= final).astype(jnp.int32),
        LBACK1: (second >= 1).astype(jnp.int32),
        LBACK2: (second >= 2).astype(jnp.int32),
        LNEXT1: (second + 1 <= final).astype(jnp.int32),
        CORE: lax.axis_index("dp"),
        AT_X: lax.axis_index("x"),
    }
    lane = lax.broadcasted_iota(jnp.int32, INFO, 1)
    found = jnp.zeros(INFO, jnp.int32)
    for n, value in values.items():
        found = jnp.where(lane == n, value, found)
    info[...] = found
    for c in copies:
        c.wait()


def forward_kernel(info, x_ref, g_ref, w_ref, tw_ref, s_ref, acc, tacc, wf, wb, tf, tb, wide, v_ref, mw):
    zero = jnp.zeros((CH, CH), BF16)
    for a in range(4):
        for q in range(3):
            rows = slice((a * 3 + q) * CH, (a * 3 + q + 1) * CH)
            for b in range(2):
                lanes = slice(b * CH, b * CH + CH)
                inside = 0 <= a - b <= 2
                wf[rows, lanes] = w_ref[a - b, q] if inside else zero
                wb[rows, lanes] = w_ref[2 - (a - b), 2 - q].T if inside else zero
    for k in range(3):
        for a in range(2):
            rows = slice((2 * k + a) * CH, (2 * k + a + 1) * CH)
            for b in range(2):
                lanes = slice(b * CH, b * CH + CH)
                tf[rows, lanes] = tw_ref[k] if a == b else zero
                tb[rows, lanes] = tw_ref[k].T if a == b else zero

    acc[...] = jnp.zeros_like(acc)
    tacc[...] = jnp.zeros_like(tacc)
    clear_edges(wide)
    mw[0 : 2 * CH] = tb[0 : 2 * CH]

    def slot(j, _):
        keep = jnp.logical_and(j == 0, jnp.logical_and(is_two(info), is_set(info, NEXT1)))
        mw[2 * CH : 4 * CH] = jnp.where(keep, tb[2 * CH : 4 * CH], jnp.zeros((2 * CH, 2 * CH), BF16))
        fill_act(wide, lambda t, n, half: x_ref[j, pl.ds(t, n), half])
        conv_to(s_ref.at[j], wide, wf)

        def upstream(t):
            at = pl.ds(t, MID)
            both = jnp.concatenate([pair(g_ref[j, at]), pair(g_ref[1, at])], axis=-1)
            v_ref[at] = dot(both, mw[...]).astype(BF16).reshape(MID, COLS, 2 * CH)

        steps(MID, upstream)
        add_spatial(acc, wide, v_ref)
        found = correlate(s_ref[j], lambda half: jnp.concatenate([g_ref[j, :, half], g_ref[1, :, half]], axis=-1))
        tacc[:, 0:CH] += found[:, 0:CH]
        tacc[:, CH : 2 * CH] += jnp.where(keep, found[:, CH : 2 * CH], 0.0)
        return 0

    lax.fori_loop(0, info[0, COUNT], slot, 0)


def mid_kernel(info, *refs, first, count):
    *hops, s, g, wf, tf, tb, sent, sh, wide, mw = refs
    if len(hops) == 2:
        hops = hops * 2
    two = is_two(info)
    even = is_set(info, EVEN)
    back = is_set(info, BACK1)
    before = halves(even, hops[0::2], hops[1::2], CUT1)
    after = halves(even, hops[1::2], hops[0::2], CUT1)
    clear_edges(wide)
    done = max(first - 1, 0)
    end = min(first + count + 1, PAIRS)
    while done < end:
        n = min(FILL - done % FILL, end - done)
        for half in range(2):
            put_act(wide, done, half, before(done, n, half))
        done += n
    sh[...] = conv(wide, wf, first, count).astype(BF16).reshape(count, COLS, 2 * CH)

    down = jnp.where(even, 0, 1)
    at = pl.ds(first, count)
    nothing = jnp.zeros((2 * CH, 2 * CH), BF16)
    mw[0 : 2 * CH] = jnp.where(back, tb[2 * CH : 4 * CH], nothing)
    mw[2 * CH : 4 * CH] = jnp.where(jnp.logical_and(back, is_set(info, NEXT1)), tb[4 * CH : 6 * CH], nothing)
    v = jnp.concatenate([pair(g[0, at]), pair(jnp.where(two, g[1, at], after(first, count)))], axis=-1)
    sent[down] = dot(v, mw[...]).astype(BF16).reshape(count, COLS, 2 * CH)

    keep1 = jnp.where(two, info[0, LNEXT1], info[0, NEXT1]) == 1
    keep2 = jnp.logical_and(keep1, jnp.where(two, info[0, LBACK1], info[0, BACK1]) == 1)
    mw[0 : 2 * CH] = jnp.where(keep1, tf[2 * CH : 4 * CH], nothing)
    mw[2 * CH : 4 * CH] = jnp.where(keep2, tf[4 * CH : 6 * CH], nothing)
    v = jnp.concatenate([flat(jnp.where(two, s[1, at], s[0, at])), flat(jnp.where(two, s[0, at], sh[...]))], axis=-1)
    sent[1 - down] = dot(v, mw[...]).astype(BF16).reshape(count, COLS, 2 * CH)


def grad_kernel(
    info, high_a, low_a, high_b, low_b, x, g, s, sent_a, sent_b, sh_a, sh_b, acc_in, tacc_in, tb, own_ref, other_ref,
    wide, v, gn, acc, tacc, both
):
    two = is_two(info)
    even = is_set(info, EVEN)
    back = is_set(info, BACK1)
    cross = jnp.logical_and(back, is_set(info, NEXT1))
    before = halves(even, (high_a, high_b), (low_a, low_b), CUT1)
    after = halves(even, (low_a, low_b), (high_a, high_b), CUT1)
    down = jnp.where(even, 0, 1)
    acc[...] = acc_in[...]
    tacc[...] = tacc_in[...]
    clear_edges(wide)
    fill_act(wide, before)
    for t in range(0, PAIRS, FILL):
        gn[pl.ds(t, FILL)] = after(t, FILL)
    for t, sent, sh in ((0, sent_a, sh_a), (CUT2, sent_b, sh_b)):
        n = sh.shape[0]
        at = pl.ds(t, n)
        v[at] = sent[down]

        def two_frames(half, at=at):
            return jnp.concatenate([g[0, at, half], jnp.where(two, g[1, at, half], gn[at, half])], axis=-1)

        found = correlate(sh[...], two_frames)
        tacc[:, CH : 2 * CH] += jnp.where(back, found[:, 0:CH], 0.0)
        tacc[:, 2 * CH : 3 * CH] += jnp.where(cross, found[:, CH : 2 * CH], 0.0)
    add_spatial(acc, wide, v)

    @pl.when(jnp.logical_and(two, is_set(info, NEXT2)))
    def _():
        fill_act(wide, lambda t, n, half: x[0, pl.ds(t, n), half])

        def up(t):
            at = pl.ds(t, MID)
            v[at] = dot(pair(gn[at]), tb[4 * CH : 6 * CH]).astype(BF16).reshape(MID, COLS, 2 * CH)

        steps(MID, up)
        add_spatial(acc, wide, v)
        tacc[:, 2 * CH : 3 * CH] += correlate(s[0], lambda half: gn[:, half])

    at_x, core = info[0, AT_X], info[0, CORE]
    for p in range(3):
        for q in range(3):
            first = (p * 3 + q) * CH
            second = ((p + 1) * 3 + q) * CH
            found = acc[0:CH, first : first + CH] + acc[CH : 2 * CH, second : second + CH]
            n = p * 3 + q
            both[n // 6, (n % 6) * CH : (n % 6 + 1) * CH] = found.T * SCALE
    for k in range(3):
        both[1, (3 + k) * CH : (4 + k) * CH] = tacc[:, k * CH : k * CH + CH] * SCALE
    for i in range(SIDE):
        source = pl.ds(pl.multiple_of(lax.rem(at_x + i, SIDE) * PIECE, PIECE), PIECE)
        own_ref[i] = both[core, source]
        other_ref[i] = both[1 - core, source]


def add_x(x, slot, out, to, sem, t, n, value):
    at = pl.ds(t, n)
    value = value.astype(BF16).astype(F32).reshape(n, COLS, 2 * CH)
    for half in range(2):
        out[at, half] = (x[slot, at, half].astype(F32) + value[:, :, half * CH : half * CH + CH]).astype(BF16)
    pltpu.make_async_copy(out.at[at], to.at[at], sem).start()


def mask_taps(mw, taps, keep1, keep2):
    nothing = jnp.zeros((2 * CH, 2 * CH), BF16)
    mw[0 : 2 * CH] = taps[0 : 2 * CH]
    mw[2 * CH : 4 * CH] = jnp.where(keep1, taps[2 * CH : 4 * CH], nothing)
    mw[4 * CH : 6 * CH] = jnp.where(keep2, taps[4 * CH : 6 * CH], nothing)


def put_upstream(wide, t, n, value):
    value = value.reshape(n, COLS, 2 * CH)
    for half in range(2):
        put_row(wide, t, half, value[:, :, half * CH : half * CH + CH])


def input_rows(wide, wb, x, g, slot, out, to, sem, first, count):
    at = pl.ds(first, count)
    back = conv(wide, wb, first, count).reshape(count, COLS, 2 * CH)
    for half in range(2):
        xv = x[slot, at, half].astype(F32)
        sig = jax.nn.sigmoid(xv)
        b = back[:, :, half * CH : half * CH + CH]
        out[at, half] = (g[slot, at, half].astype(F32) + b * (sig * (1.0 + xv * (1.0 - sig)))).astype(BF16)
    pltpu.make_async_copy(out.at[at], to.at[at], sem).start()


def early_out_kernel(info, x, s, sh_a, sh_b, tf, after, out_any, token, mw, out, sem):
    to = out_any.at[1]

    @pl.when(is_two(info))
    def _():
        mask_taps(mw, tf, is_set(info, LBACK1), is_set(info, LBACK2))
        for t, sh in ((0, sh_a), (CUT2, sh_b)):
            n = sh.shape[0]
            at = pl.ds(t, n)
            v = jnp.concatenate([flat(s[1, at]), flat(s[0, at]), flat(sh[...])], axis=-1)
            add_x(x, 1, out, to, sem, t, n, dot(v, mw[...]))

    @pl.when(jnp.logical_not(is_two(info)))
    def _():
        out[...] = jnp.zeros_like(out)
        pltpu.make_async_copy(out, to, sem).start()

    token[...] = jnp.zeros_like(token)
    pltpu.make_async_copy(out, to, sem).wait()


def early_in_kernel(info, x, g, high_a, low_a, high_b, low_b, wb, tb, after, out_any, token, mw, wide, out, sem):
    two = is_two(info)
    coming = halves(is_set(info, EVEN), (low_a, low_b), (high_a, high_b), CUT1)

    @pl.when(two)
    def _():
        mask_taps(mw, tb, is_set(info, NEXT1), is_set(info, NEXT2))
        clear_edges(wide)
        for t in range(0, PAIRS, FILL):
            at = pl.ds(t, FILL)
            v = jnp.concatenate([pair(g[0, at]), pair(g[1, at]), pair(coming(t, FILL))], axis=-1)
            put_upstream(wide, t, FILL, dot(v, mw[...]))
        for t in range(0, PAIRS, MID):
            input_rows(wide, wb, x, g, 0, out, out_any.at[0], sem, t, MID)

    @pl.when(jnp.logical_not(two))
    def _():
        out[...] = jnp.zeros_like(out)
        pltpu.make_async_copy(out, out_any.at[1], sem).start()

    token[...] = jnp.zeros_like(token)
    pltpu.make_async_copy(out, out_any.at[1], sem).wait()


def output_kernel(info, x, s, high_a, low_a, high_b, low_b, tf, early, out_any, token, out, sem):
    ahead = halves(is_set(info, EVEN), (high_a, high_b), (low_a, low_b), CUT2)
    to = out_any.at[0]
    for t, n in ((0, CUT2), (CUT2, PAIRS - CUT2)):
        value = dot(flat(s[0, pl.ds(t, n)]), tf[0 : 2 * CH]) + flat(ahead(t, n)).astype(F32)
        add_x(x, 0, out, to, sem, t, n, value)
    token[...] = jnp.zeros_like(token)
    pltpu.make_async_copy(out, to, sem).wait()


def input_kernel(info, x, g, high_a, low_a, high_b, low_b, wb, tb, early, out_any, token, wide, out, sem, *, first):
    last = jnp.where(is_two(info), 1, 0)
    share = halves(is_set(info, EVEN), (low_a, low_b), (high_a, high_b), CUT2)
    to = out_any.at[last]
    clear_edges(wide)
    done = max(first - 1, 0)
    end = min(first + MID + 1, PAIRS)
    while done < end:
        n = min(FILL - done % FILL, end - done)
        value = dot(pair(g[last, pl.ds(done, n)]), tb[0 : 2 * CH]) + flat(share(done, n)).astype(F32)
        put_upstream(wide, done, n, value)
        done += n
    input_rows(wide, wb, x, g, last, out, to, sem, first, MID)
    token[...] = jnp.zeros_like(token)
    rows = pl.ds(first, MID)
    pltpu.make_async_copy(out.at[rows], to.at[rows], sem).wait()


def hold_kernel(*refs):
    pass


def place_kernel(info, mine, theirs, spatial, temporal_out):
    at_x, core = info[0, AT_X], info[0, CORE]
    for half in range(2):
        for i in range(SIDE):
            n = lax.rem(at_x + SIDE - i, SIDE)
            piece = jnp.where(core == half, mine[n], theirs[n]).astype(F32)
            row = half * HALF + i * PIECE
            if row < 9 * CH:
                spatial[row : row + PIECE] = piece
            else:
                temporal_out[row - 9 * CH : row - 9 * CH + PIECE] = piece


FRAME = (PAIRS, 2, COLS, CH)
S_SHAPE = (PAIRS, COLS, 2 * CH)
WIDE = pltpu.VMEM((PAIRS + 1, COLS, 6 * CH), BF16)
VALUES = pltpu.VMEM(S_SHAPE, BF16)
W_SHAPE = (12 * CH, 2 * CH)
T_SHAPE = (6 * CH, 2 * CH)
TAPS = pltpu.VMEM(T_SHAPE, BF16)
TAPS2 = pltpu.VMEM((4 * CH, 2 * CH), BF16)
ACC = (2 * CH, 12 * CH)
TACC = (CH, 3 * CH)
PIECES = (SIDE, PIECE, CH)
VMEM = pl.BlockSpec(memory_space=pltpu.VMEM)
ANY = pl.BlockSpec(memory_space=pl.ANY)
HBM = pl.BlockSpec(memory_space=pltpu.HBM)
FRAME1 = pltpu.VMEM(FRAME, BF16)
SEM = pltpu.SemaphoreType.DMA
def shape(s, d=BF16):
    return jax.ShapeDtypeStruct(s, d)


def in_hbm(value):
    return pltpu.with_memory_space_constraint(value, pltpu.HBM)


def call(kernel, in_specs, outs, scratch, name, out_specs=None, aliases=None):
    return pl.pallas_call(
        kernel,
        in_specs=in_specs,
        out_specs=out_specs or [VMEM] * len(outs),
        out_shape=outs,
        scratch_shapes=scratch,
        input_output_aliases=aliases or {},
        compiler_params=pltpu.CompilerParams(vmem_limit_bytes=VMEM_BYTES),
        cost_estimate=pl.CostEstimate(flops=1, transcendentals=0, bytes_accessed=1),
        name=name,
    )


def shifts(value, axis, k):
    return lax.ppermute(value, axis, [(i, (i + k) % SIDE) for i in range(SIDE)])


def to_sum(parts, axis):
    return [parts[0]] + [shifts(parts[k], axis, k) for k in range(1, SIDE)]


def gather(part, axis):
    return [part] + [shifts(part, axis, k) for k in range(1, SIDE)]


def split_call(name, n_sum, n_out, out, n_after=0, kind=F32):
    def kernel(*refs):
        ins, outs = refs[:n_sum], refs[n_sum + n_after :]
        for n, out_ref in enumerate(outs):
            v = [(r[n] if n_out > 1 else r[...]).astype(F32) for r in ins]
            total = v[0] + v[1] if n_sum == 2 else (v[0] + v[2]) + (v[1] + v[3])
            out_ref[...] = total.astype(kind)

    return call(kernel, [VMEM] * n_sum + [ANY] * n_after, [shape(out, kind)] * n_out, [], name)


def stack_call(name, out, n_after):
    def kernel(*refs):
        for n in range(SIDE):
            refs[-1][n] = refs[n][...]

    run = call(kernel, [VMEM] * SIDE + [ANY] * n_after, [shape(out)], [], name)
    return lambda *a: run(*a)[0]


def local(latents, cotangent, frame_counts, spatial_weight, temporal_weight):
    axes = ("x", "y", "z")
    x = latents.reshape((2,) + FRAME)
    g = cotangent.reshape((2,) + FRAME)
    lows = range(0, N_SP, 2)
    low = [(i, i + 1) for i in lows] + [(i + 1, i) for i in lows]
    high = [(i + 1, (i + 2) % N_SP) for i in lows] + [((i + 2) % N_SP, i + 1) for i in lows]
    swap = [(0, 1), (1, 0)]

    parts = [shape((n, 2, COLS, CH)) for n in (CUT1, CUT1, PAIRS - CUT1, PAIRS - CUT1)]
    info, *sent = call(
        prep_kernel, [VMEM, HBM, HBM], [shape(INFO, jnp.int32)] + parts, [SEM((4,))], "prep", [VMEM] + [ANY] * 4
    )(frame_counts, in_hbm(x), in_hbm(g))

    def hop(for_high, for_low):
        return lax.ppermute(for_high, axes, high), lax.ppermute(for_low, axes, low)

    hop1_a = hop(*sent[0:2])
    hop1_b = hop(*sent[2:4])
    hop1 = hop1_a + hop1_b

    s, acc, tacc, wf, wb, tf, tb = call(
        forward_kernel,
        [VMEM] * 5,
        [shape((2,) + S_SHAPE), shape(ACC, F32), shape(TACC, F32), shape(W_SHAPE), shape(W_SHAPE), shape(T_SHAPE), shape(T_SHAPE)],
        [WIDE, VALUES, TAPS2],
        "forward",
    )(info, x, g, spatial_weight, temporal_weight)

    def mid(first, count, hops):
        return call(
            functools.partial(mid_kernel, first=first, count=count),
            [VMEM] * (6 + len(hops)),
            [shape((2, count) + S_SHAPE[1:]), shape((count,) + S_SHAPE[1:])],
            [WIDE, TAPS2],
            "mid",
        )(info, *hops, s, g, wf, tf, tb)

    sent_a, sh_a = mid(0, CUT2, hop1_a)
    hop2_a = hop(sent_a[0], sent_a[1])
    sent_b, sh_b = mid(CUT2, PAIRS - CUT2, hop1)
    hop2_b = hop(sent_b[0], sent_b[1])
    hop2 = hop2_a + hop2_b

    own, other = call(
        grad_kernel,
        [VMEM] * 15,
        [shape(PIECES, F32), shape(PIECES, F32)],
        [WIDE, VALUES, FRAME1, pltpu.VMEM(ACC, F32), pltpu.VMEM(TACC, F32), pltpu.VMEM((2, HALF, CH), F32)],
        "grads",
    )(info, *hop1, x, g, s, sent_a, sent_b, sh_a, sh_b, acc, tacc, tb)

    other = call(hold_kernel, [ANY] * 3, [shape(PIECES, F32)], [], "hold", [ANY], {2: 0})(*hop2_a, other)[0]
    chunks = split_call("core_sum", 2, SIDE, PIECES[1:])(own, lax.ppermute(other, "dp", swap))
    frames = [pltpu.HBM((2,) + FRAME, BF16), shape((8, CH), F32)]
    early_out, done_a = call(
        early_out_kernel, [VMEM] * 6 + [ANY], frames, [TAPS, FRAME1, SEM], "early_out", [ANY, VMEM]
    )(info, x, s, sh_a, sh_b, tf, chunks[0])
    early_in, done_b = call(
        early_in_kernel, [VMEM] * 9 + [ANY], frames, [TAPS, WIDE, FRAME1, SEM], "early_in", [ANY, VMEM]
    )(info, x, g, *hop1, wb, tb, chunks[0])
    part = split_call("x_sum", SIDE, 1, PIECES[1:], 2, BF16)(*to_sum(chunks, "x"), done_a, done_b)[0]
    block_out, done_c = call(
        output_kernel, [VMEM] * 8 + [ANY], frames, [FRAME1, SEM], "output", [ANY, VMEM], {8: 0}
    )(info, x, s, *hop2, tf, in_hbm(early_out))
    part = split_call("y_sum", SIDE, 1, PIECES[1:], 1, BF16)(*gather(part, "y"), done_c)[0]

    def input_half(first, so_far):
        return call(
            functools.partial(input_kernel, first=first),
            [VMEM] * 9 + [ANY],
            frames,
            [WIDE, FRAME1, SEM],
            "input_grad",
            [ANY, VMEM],
            {9: 0},
        )(info, x, g, *hop2, wb, tb, in_hbm(so_far))

    input_grad, done_d = input_half(0, early_in)
    part = split_call("z_sum", SIDE, 1, PIECES[1:], 1, BF16)(*gather(part, "z"), done_d)[0]
    input_grad, done_e = input_half(PAIRS // 2, input_grad)
    own = stack_call("x_stack", PIECES, 1)(*gather(part, "x"), done_e)
    theirs = lax.ppermute(own, "dp", swap)
    spatial_grad, temporal_grad = call(
        place_kernel, [VMEM, VMEM, VMEM], [shape((9 * CH, CH), F32), shape((3 * CH, CH), F32)], [], "place"
    )(info, own, theirs)
    return (
        block_out.reshape(latents.shape),
        input_grad.reshape(latents.shape),
        spatial_grad.reshape(3, 3, CH, CH),
        temporal_grad.reshape(3, CH, CH),
    )


def solution(mesh):
    chips = Mesh(mesh.devices.reshape(2, SIDE, SIDE, SIDE), ("dp", "x", "y", "z"))
    held = P(("dp", "x", "y", "z"), None, None, None)
    return jax.shard_map(
        local,
        mesh=chips,
        in_specs=(held, held, P("dp", None), P(), P()),
        out_specs=(held, held, P(), P()),
        check_vma=False,
    )
```

```python
import functools

import jax
import jax.numpy as jnp
from jax import lax
from jax.experimental import pallas as pl
from jax.experimental.pallas import tpu as pltpu
from jax.sharding import Mesh
from jax.sharding import PartitionSpec as P

FRAMES = 9
CLIPS = 8
CH = 128
ROWS = 64
COLS = 64
N_SP = 64
SIDE = 4
PAIRS = ROWS // 2
F32 = jnp.float32
BF16 = jnp.bfloat16
VMEM_BYTES = 24 * 1024 * 1024
SCALE = float(2 * CLIPS * FRAMES * ROWS * COLS) ** (-0.5)
HALF = 6 * CH
PIECE = HALF // SIDE

COUNT, EVEN, BACK1, NEXT1, NEXT2, LBACK1, LBACK2, LNEXT1, CORE, AT_X = range(10)
INFO = (8, 128)

FILL = 8
MID = 16
FULL = 32
CUT1 = 16
CUT2 = 15


def dot(a, b):
    return jnp.dot(a, b, preferred_element_type=F32)


def dot_t(a, b):
    return lax.dot_general(a, b, (((0,), (0,)), ((), ())), preferred_element_type=F32)


def steps(block, body):
    def one(n, _):
        body(n * block)
        return 0

    lax.fori_loop(0, PAIRS // block, one, 0)


def clear_edges(wide):
    wide[0, :, 0 : 3 * CH] = jnp.zeros((COLS, 3 * CH), BF16)
    wide[PAIRS, :, 3 * CH : 6 * CH] = jnp.zeros((COLS, 3 * CH), BF16)


def put_row(wide, t, half, a):
    col = lax.broadcasted_iota(jnp.int32, a.shape, 1)
    before = jnp.where(col == 0, 0.0, pltpu.roll(a, 1, 1))
    after = jnp.where(col == COLS - 1, 0.0, pltpu.roll(a, COLS - 1, 1))
    at = pl.ds(t + half, a.shape[0])
    base = 0 if half else 3 * CH
    wide[at, :, base : base + CH] = before.astype(BF16)
    wide[at, :, base + CH : base + 2 * CH] = a.astype(BF16)
    wide[at, :, base + 2 * CH : base + 3 * CH] = after.astype(BF16)


def put_act(wide, t, half, x):
    x = x.astype(F32)
    put_row(wide, t, half, x * jax.nn.sigmoid(x))


def fill_act(wide, rows, first=0, count=PAIRS):
    for t in range(first, first + count, FILL):
        for half in range(2):
            put_act(wide, t, half, rows(t, FILL, half))


def windows(wide, t, block):
    low = wide[pl.ds(t, block)].reshape(block * COLS, 6 * CH)
    high = wide[pl.ds(t + 1, block)].reshape(block * COLS, 6 * CH)
    return low, high


def conv(wide, w_ref, t, block):
    low, high = windows(wide, t, block)
    return dot(low, w_ref[0 : 6 * CH, :]) + dot(high, w_ref[6 * CH : 12 * CH, :])


def conv_to(out_ref, wide, w_ref):
    def body(t):
        out_ref[pl.ds(t, FULL)] = conv(wide, w_ref, t, FULL).astype(BF16).reshape(FULL, COLS, 2 * CH)

    steps(FULL, body)


def pair(v):
    return jnp.concatenate([v[:, 0], v[:, 1]], axis=-1).reshape(v.shape[0] * COLS, 2 * CH)


def flat(v):
    return v.reshape(v.shape[0] * COLS, 2 * CH)


def add_spatial(acc, wide, v_ref):
    def body(t):
        low, high = windows(wide, t, FULL)
        v = flat(v_ref[pl.ds(t, FULL)])
        acc[:, 0 : 6 * CH] += dot_t(v, low)
        acc[:, 6 * CH : 12 * CH] += dot_t(v, high)

    steps(FULL, body)


def correlate(s, gs):
    total = None
    for half in range(2):
        a = s[:, :, half * CH : half * CH + CH].reshape(s.shape[0] * COLS, CH)
        b = gs(half)
        one = dot_t(a, b.reshape(s.shape[0] * COLS, b.shape[-1]))
        total = one if total is None else total + one
    return total


def copy_either(first, a, b, sem):
    @pl.when(first)
    def _():
        pltpu.make_async_copy(*a, sem).start()

    @pl.when(jnp.logical_not(first))
    def _():
        pltpu.make_async_copy(*b, sem).start()

    return pltpu.make_async_copy(*a, sem)


def is_two(info):
    return info[0, COUNT] == 2


def is_set(info, n):
    return info[0, n] == 1


def either(first, a, b):
    return lambda *at: jnp.where(first, a[at], b[at])


def halves(first, a, b, cut):
    parts = (either(first, a[0], b[0]), either(first, a[1], b[1]))

    def read(t, n, *at):
        found = []
        if t < cut:
            found.append(parts[0](pl.ds(t, min(n, cut - t)), *at))
        if t + n > cut:
            start = max(t, cut)
            found.append(parts[1](pl.ds(start - cut, t + n - start), *at))
        return found[0] if len(found) == 1 else jnp.concatenate(found, axis=0)

    return read


def prep_kernel(counts, x_hbm, g_hbm, info, high_a, low_a, high_b, low_b, sems):
    here = (lax.axis_index("x") * SIDE + lax.axis_index("y")) * SIDE + lax.axis_index("z")
    even = here % 2 == 0

    top, bottom = pl.ds(0, CUT1), pl.ds(CUT1, PAIRS - CUT1)

    def put(source, slot, for_high, n):
        a = copy_either(for_high, (source.at[slot, top], high_a), (source.at[slot, top], low_a), sems.at[n])
        b = copy_either(for_high, (source.at[slot, bottom], high_b), (source.at[slot, bottom], low_b), sems.at[n + 1])
        return [a, b]

    copies = put(g_hbm, 0, even, 0)
    c = counts[...].astype(F32)
    order = lax.broadcasted_iota(jnp.int32, c.shape, 1)
    start = jnp.sum(jnp.where(order < here, c, 0.0)).astype(jnp.int32)
    count = jnp.sum(jnp.where(order == here, c, 0.0)).astype(jnp.int32)
    copies += put(x_hbm, jnp.where(count == 2, 1, 0), jnp.logical_not(even), 2)
    first = start % FRAMES
    second = (first + 1) % FRAMES
    final = FRAMES - 1
    values = {
        COUNT: count,
        EVEN: even.astype(jnp.int32),
        BACK1: (first >= 1).astype(jnp.int32),
        NEXT1: (first + 1 <= final).astype(jnp.int32),
        NEXT2: (first + 2 <= final).astype(jnp.int32),
        LBACK1: (second >= 1).astype(jnp.int32),
        LBACK2: (second >= 2).astype(jnp.int32),
        LNEXT1: (second + 1 <= final).astype(jnp.int32),
        CORE: lax.axis_index("dp"),
        AT_X: lax.axis_index("x"),
    }
    lane = lax.broadcasted_iota(jnp.int32, INFO, 1)
    found = jnp.zeros(INFO, jnp.int32)
    for n, value in values.items():
        found = jnp.where(lane == n, value, found)
    info[...] = found
    for c in copies:
        c.wait()


def forward_kernel(info, x_ref, g_ref, w_ref, tw_ref, s_ref, acc, tacc, wf, wb, tf, tb, wide, v_ref, mw):
    zero = jnp.zeros((CH, CH), BF16)
    for a in range(4):
        for q in range(3):
            rows = slice((a * 3 + q) * CH, (a * 3 + q + 1) * CH)
            for b in range(2):
                lanes = slice(b * CH, b * CH + CH)
                inside = 0 <= a - b <= 2
                wf[rows, lanes] = w_ref[a - b, q] if inside else zero
                wb[rows, lanes] = w_ref[2 - (a - b), 2 - q].T if inside else zero
    for k in range(3):
        for a in range(2):
            rows = slice((2 * k + a) * CH, (2 * k + a + 1) * CH)
            for b in range(2):
                lanes = slice(b * CH, b * CH + CH)
                tf[rows, lanes] = tw_ref[k] if a == b else zero
                tb[rows, lanes] = tw_ref[k].T if a == b else zero

    acc[...] = jnp.zeros_like(acc)
    tacc[...] = jnp.zeros_like(tacc)
    clear_edges(wide)
    mw[0 : 2 * CH] = tb[0 : 2 * CH]

    def slot(j, _):
        keep = jnp.logical_and(j == 0, jnp.logical_and(is_two(info), is_set(info, NEXT1)))
        mw[2 * CH : 4 * CH] = jnp.where(keep, tb[2 * CH : 4 * CH], jnp.zeros((2 * CH, 2 * CH), BF16))
        fill_act(wide, lambda t, n, half: x_ref[j, pl.ds(t, n), half])
        conv_to(s_ref.at[j], wide, wf)

        def upstream(t):
            at = pl.ds(t, MID)
            both = jnp.concatenate([pair(g_ref[j, at]), pair(g_ref[1, at])], axis=-1)
            v_ref[at] = dot(both, mw[...]).astype(BF16).reshape(MID, COLS, 2 * CH)

        steps(MID, upstream)
        add_spatial(acc, wide, v_ref)
        found = correlate(s_ref[j], lambda half: jnp.concatenate([g_ref[j, :, half], g_ref[1, :, half]], axis=-1))
        tacc[:, 0:CH] += found[:, 0:CH]
        tacc[:, CH : 2 * CH] += jnp.where(keep, found[:, CH : 2 * CH], 0.0)
        return 0

    lax.fori_loop(0, info[0, COUNT], slot, 0)


def mid_kernel(info, *refs, first, count):
    *hops, s, g, wf, tf, tb, sent, sh, wide, mw = refs
    if len(hops) == 2:
        hops = hops * 2
    two = is_two(info)
    even = is_set(info, EVEN)
    back = is_set(info, BACK1)
    before = halves(even, hops[0::2], hops[1::2], CUT1)
    after = halves(even, hops[1::2], hops[0::2], CUT1)
    end = first + count
    if first == 0:
        wide[0, :, 0 : 3 * CH] = jnp.zeros((COLS, 3 * CH), BF16)
    else:
        put_act(wide, -1, 1, before(first - 1, 1, 1))
    for t in range(first, end, FILL):
        n = min(FILL, end - t)
        for half in range(2):
            put_act(wide, t - first, half, before(t, n, half))
    if end == PAIRS:
        wide[count, :, 3 * CH : 6 * CH] = jnp.zeros((COLS, 3 * CH), BF16)
    else:
        put_act(wide, count, 0, before(end, 1, 0))
    sh[...] = conv(wide, wf, 0, count).astype(BF16).reshape(count, COLS, 2 * CH)

    down = jnp.where(even, 0, 1)
    at = pl.ds(first, count)
    nothing = jnp.zeros((2 * CH, 2 * CH), BF16)
    mw[0 : 2 * CH] = jnp.where(back, tb[2 * CH : 4 * CH], nothing)
    mw[2 * CH : 4 * CH] = jnp.where(jnp.logical_and(back, is_set(info, NEXT1)), tb[4 * CH : 6 * CH], nothing)
    v = jnp.concatenate([pair(g[0, at]), pair(jnp.where(two, g[1, at], after(first, count)))], axis=-1)
    sent[down] = dot(v, mw[...]).astype(BF16).reshape(count, COLS, 2 * CH)

    keep1 = jnp.where(two, info[0, LNEXT1], info[0, NEXT1]) == 1
    keep2 = jnp.logical_and(keep1, jnp.where(two, info[0, LBACK1], info[0, BACK1]) == 1)
    mw[0 : 2 * CH] = jnp.where(keep1, tf[2 * CH : 4 * CH], nothing)
    mw[2 * CH : 4 * CH] = jnp.where(keep2, tf[4 * CH : 6 * CH], nothing)
    v = jnp.concatenate([flat(jnp.where(two, s[1, at], s[0, at])), flat(jnp.where(two, s[0, at], sh[...]))], axis=-1)
    sent[1 - down] = dot(v, mw[...]).astype(BF16).reshape(count, COLS, 2 * CH)


def grad_kernel(
    info, high_a, low_a, high_b, low_b, x, g, s, sent_a, sent_b, sh_a, sh_b, wide_a, wide_b, acc_in, tacc_in, tb,
    own_ref, other_ref, wide, v, gn, acc, tacc, both
):
    two = is_two(info)
    even = is_set(info, EVEN)
    back = is_set(info, BACK1)
    cross = jnp.logical_and(back, is_set(info, NEXT1))
    after = halves(even, (low_a, low_b), (high_a, high_b), CUT1)
    down = jnp.where(even, 0, 1)
    acc[...] = acc_in[...]
    tacc[...] = tacc_in[...]
    for t in range(0, PAIRS, FILL):
        gn[pl.ds(t, FILL)] = after(t, FILL)
    for t, sent, sh, part in ((0, sent_a, sh_a, wide_a), (CUT2, sent_b, sh_b, wide_b)):
        n = sh.shape[0]
        at = pl.ds(t, n)

        def two_frames(half, at=at):
            return jnp.concatenate([g[0, at, half], jnp.where(two, g[1, at, half], gn[at, half])], axis=-1)

        found = correlate(sh[...], two_frames)
        tacc[:, CH : 2 * CH] += jnp.where(back, found[:, 0:CH], 0.0)
        tacc[:, 2 * CH : 3 * CH] += jnp.where(cross, found[:, CH : 2 * CH], 0.0)
        low, high = windows(part, 0, n)
        value = flat(sent[down])
        acc[:, 0 : 6 * CH] += dot_t(value, low)
        acc[:, 6 * CH : 12 * CH] += dot_t(value, high)

    @pl.when(jnp.logical_and(two, is_set(info, NEXT2)))
    def _():
        clear_edges(wide)
        fill_act(wide, lambda t, n, half: x[0, pl.ds(t, n), half])

        def up(t):
            at = pl.ds(t, MID)
            v[at] = dot(pair(gn[at]), tb[4 * CH : 6 * CH]).astype(BF16).reshape(MID, COLS, 2 * CH)

        steps(MID, up)
        add_spatial(acc, wide, v)
        tacc[:, 2 * CH : 3 * CH] += correlate(s[0], lambda half: gn[:, half])

    at_x, core = info[0, AT_X], info[0, CORE]
    for p in range(3):
        for q in range(3):
            first = (p * 3 + q) * CH
            second = ((p + 1) * 3 + q) * CH
            found = acc[0:CH, first : first + CH] + acc[CH : 2 * CH, second : second + CH]
            n = p * 3 + q
            both[n // 6, (n % 6) * CH : (n % 6 + 1) * CH] = found.T * SCALE
    for k in range(3):
        both[1, (3 + k) * CH : (4 + k) * CH] = tacc[:, k * CH : k * CH + CH] * SCALE
    for i in range(SIDE):
        source = pl.ds(pl.multiple_of(lax.rem(at_x + i, SIDE) * PIECE, PIECE), PIECE)
        own_ref[i] = both[core, source]
        other_ref[i] = both[1 - core, source]


def add_x(x, slot, out, to, sem, t, n, value):
    at = pl.ds(t, n)
    value = value.astype(BF16).astype(F32).reshape(n, COLS, 2 * CH)
    for half in range(2):
        out[at, half] = (x[slot, at, half].astype(F32) + value[:, :, half * CH : half * CH + CH]).astype(BF16)
    pltpu.make_async_copy(out.at[at], to.at[at], sem).start()


def mask_taps(mw, taps, keep1, keep2):
    nothing = jnp.zeros((2 * CH, 2 * CH), BF16)
    mw[0 : 2 * CH] = taps[0 : 2 * CH]
    mw[2 * CH : 4 * CH] = jnp.where(keep1, taps[2 * CH : 4 * CH], nothing)
    mw[4 * CH : 6 * CH] = jnp.where(keep2, taps[4 * CH : 6 * CH], nothing)


def put_upstream(wide, t, n, value):
    value = value.reshape(n, COLS, 2 * CH)
    for half in range(2):
        put_row(wide, t, half, value[:, :, half * CH : half * CH + CH])


def input_rows(wide, wb, x, g, slot, out, to, sem, first, count):
    at = pl.ds(first, count)
    back = conv(wide, wb, first, count).reshape(count, COLS, 2 * CH)
    for half in range(2):
        xv = x[slot, at, half].astype(F32)
        sig = jax.nn.sigmoid(xv)
        b = back[:, :, half * CH : half * CH + CH]
        out[at, half] = (g[slot, at, half].astype(F32) + b * (sig * (1.0 + xv * (1.0 - sig)))).astype(BF16)
    pltpu.make_async_copy(out.at[at], to.at[at], sem).start()


def early_out_kernel(info, x, s, sh_a, sh_b, tf, after, out_any, token, mw, out, sem):
    to = out_any.at[1]

    @pl.when(is_two(info))
    def _():
        mask_taps(mw, tf, is_set(info, LBACK1), is_set(info, LBACK2))
        for t, sh in ((0, sh_a), (CUT2, sh_b)):
            n = sh.shape[0]
            at = pl.ds(t, n)
            v = jnp.concatenate([flat(s[1, at]), flat(s[0, at]), flat(sh[...])], axis=-1)
            add_x(x, 1, out, to, sem, t, n, dot(v, mw[...]))

    @pl.when(jnp.logical_not(is_two(info)))
    def _():
        out[...] = jnp.zeros_like(out)
        pltpu.make_async_copy(out, to, sem).start()

    token[...] = jnp.zeros_like(token)
    pltpu.make_async_copy(out, to, sem).wait()


def early_in_kernel(info, x, g, high_a, low_a, high_b, low_b, wb, tb, after, out_any, token, mw, wide, out, sem):
    two = is_two(info)
    coming = halves(is_set(info, EVEN), (low_a, low_b), (high_a, high_b), CUT1)

    @pl.when(two)
    def _():
        mask_taps(mw, tb, is_set(info, NEXT1), is_set(info, NEXT2))
        clear_edges(wide)
        for t in range(0, PAIRS, FILL):
            at = pl.ds(t, FILL)
            v = jnp.concatenate([pair(g[0, at]), pair(g[1, at]), pair(coming(t, FILL))], axis=-1)
            put_upstream(wide, t, FILL, dot(v, mw[...]))
        for t in range(0, PAIRS, MID):
            input_rows(wide, wb, x, g, 0, out, out_any.at[0], sem, t, MID)

    @pl.when(jnp.logical_not(two))
    def _():
        out[...] = jnp.zeros_like(out)
        pltpu.make_async_copy(out, out_any.at[1], sem).start()

    token[...] = jnp.zeros_like(token)
    pltpu.make_async_copy(out, out_any.at[1], sem).wait()


def output_kernel(info, x, s, high_a, low_a, high_b, low_b, tf, early, out_any, token, out, sem):
    ahead = halves(is_set(info, EVEN), (high_a, high_b), (low_a, low_b), CUT2)
    to = out_any.at[0]
    for t, n in ((0, CUT2), (CUT2, PAIRS - CUT2)):
        value = dot(flat(s[0, pl.ds(t, n)]), tf[0 : 2 * CH]) + flat(ahead(t, n)).astype(F32)
        add_x(x, 0, out, to, sem, t, n, value)
    token[...] = jnp.zeros_like(token)
    pltpu.make_async_copy(out, to, sem).wait()


def input_kernel(info, x, g, high_a, low_a, high_b, low_b, wb, tb, early, out_any, token, wide, out, sem, *, first):
    last = jnp.where(is_two(info), 1, 0)
    share = halves(is_set(info, EVEN), (low_a, low_b), (high_a, high_b), CUT2)
    to = out_any.at[last]
    clear_edges(wide)
    done = max(first - 1, 0)
    end = min(first + MID + 1, PAIRS)
    while done < end:
        n = min(FILL - done % FILL, end - done)
        value = dot(pair(g[last, pl.ds(done, n)]), tb[0 : 2 * CH]) + flat(share(done, n)).astype(F32)
        put_upstream(wide, done, n, value)
        done += n
    input_rows(wide, wb, x, g, last, out, to, sem, first, MID)
    token[...] = jnp.zeros_like(token)
    rows = pl.ds(first, MID)
    pltpu.make_async_copy(out.at[rows], to.at[rows], sem).wait()


def hold_kernel(*refs):
    pass


def place_kernel(info, mine, theirs, spatial, temporal_out):
    at_x, core = info[0, AT_X], info[0, CORE]
    for half in range(2):
        for i in range(SIDE):
            n = lax.rem(at_x + SIDE - i, SIDE)
            piece = jnp.where(core == half, mine[n], theirs[n]).astype(F32)
            row = half * HALF + i * PIECE
            if row < 9 * CH:
                spatial[row : row + PIECE] = piece
            else:
                temporal_out[row - 9 * CH : row - 9 * CH + PIECE] = piece


FRAME = (PAIRS, 2, COLS, CH)
S_SHAPE = (PAIRS, COLS, 2 * CH)
WIDE = pltpu.VMEM((PAIRS + 1, COLS, 6 * CH), BF16)
VALUES = pltpu.VMEM(S_SHAPE, BF16)
W_SHAPE = (12 * CH, 2 * CH)
T_SHAPE = (6 * CH, 2 * CH)
TAPS = pltpu.VMEM(T_SHAPE, BF16)
TAPS2 = pltpu.VMEM((4 * CH, 2 * CH), BF16)
ACC = (2 * CH, 12 * CH)
TACC = (CH, 3 * CH)
PIECES = (SIDE, PIECE, CH)
VMEM = pl.BlockSpec(memory_space=pltpu.VMEM)
ANY = pl.BlockSpec(memory_space=pl.ANY)
HBM = pl.BlockSpec(memory_space=pltpu.HBM)
FRAME1 = pltpu.VMEM(FRAME, BF16)
SEM = pltpu.SemaphoreType.DMA
def shape(s, d=BF16):
    return jax.ShapeDtypeStruct(s, d)


def in_hbm(value):
    return pltpu.with_memory_space_constraint(value, pltpu.HBM)


def call(kernel, in_specs, outs, scratch, name, out_specs=None, aliases=None):
    return pl.pallas_call(
        kernel,
        in_specs=in_specs,
        out_specs=out_specs or [VMEM] * len(outs),
        out_shape=outs,
        scratch_shapes=scratch,
        input_output_aliases=aliases or {},
        compiler_params=pltpu.CompilerParams(vmem_limit_bytes=VMEM_BYTES),
        cost_estimate=pl.CostEstimate(flops=1, transcendentals=0, bytes_accessed=1),
        name=name,
    )


def shifts(value, axis, k):
    return lax.ppermute(value, axis, [(i, (i + k) % SIDE) for i in range(SIDE)])


def to_sum(parts, axis):
    return [parts[0]] + [shifts(parts[k], axis, k) for k in range(1, SIDE)]


def gather(part, axis):
    return [part] + [shifts(part, axis, k) for k in range(1, SIDE)]


def split_call(name, n_sum, n_out, out, n_after=0, kind=F32):
    def kernel(*refs):
        ins, outs = refs[:n_sum], refs[n_sum + n_after :]
        for n, out_ref in enumerate(outs):
            v = [(r[n] if n_out > 1 else r[...]).astype(F32) for r in ins]
            total = v[0] + v[1] if n_sum == 2 else (v[0] + v[2]) + (v[1] + v[3])
            out_ref[...] = total.astype(kind)

    return call(kernel, [VMEM] * n_sum + [ANY] * n_after, [shape(out, kind)] * n_out, [], name)


def stack_call(name, out, n_after):
    def kernel(*refs):
        for n in range(SIDE):
            refs[-1][n] = refs[n][...]

    run = call(kernel, [VMEM] * SIDE + [ANY] * n_after, [shape(out)], [], name)
    return lambda *a: run(*a)[0]


def local(latents, cotangent, frame_counts, spatial_weight, temporal_weight):
    axes = ("x", "y", "z")
    x = latents.reshape((2,) + FRAME)
    g = cotangent.reshape((2,) + FRAME)
    lows = range(0, N_SP, 2)
    low = [(i, i + 1) for i in lows] + [(i + 1, i) for i in lows]
    high = [(i + 1, (i + 2) % N_SP) for i in lows] + [((i + 2) % N_SP, i + 1) for i in lows]
    swap = [(0, 1), (1, 0)]

    parts = [shape((n, 2, COLS, CH)) for n in (CUT1, CUT1, PAIRS - CUT1, PAIRS - CUT1)]
    info, *sent = call(
        prep_kernel, [VMEM, HBM, HBM], [shape(INFO, jnp.int32)] + parts, [SEM((4,))], "prep", [VMEM] + [ANY] * 4
    )(frame_counts, in_hbm(x), in_hbm(g))

    def hop(for_high, for_low):
        return lax.ppermute(for_high, axes, high), lax.ppermute(for_low, axes, low)

    hop1_a = hop(*sent[0:2])
    hop1_b = hop(*sent[2:4])
    hop1 = hop1_a + hop1_b

    s, acc, tacc, wf, wb, tf, tb = call(
        forward_kernel,
        [VMEM] * 5,
        [shape((2,) + S_SHAPE), shape(ACC, F32), shape(TACC, F32), shape(W_SHAPE), shape(W_SHAPE), shape(T_SHAPE), shape(T_SHAPE)],
        [WIDE, VALUES, TAPS2],
        "forward",
    )(info, x, g, spatial_weight, temporal_weight)

    def mid(first, count, hops):
        return call(
            functools.partial(mid_kernel, first=first, count=count),
            [VMEM] * (6 + len(hops)),
            [shape((2, count) + S_SHAPE[1:]), shape((count,) + S_SHAPE[1:]), shape((count + 1, COLS, 6 * CH))],
            [TAPS2],
            "mid",
        )(info, *hops, s, g, wf, tf, tb)

    sent_a, sh_a, wide_a = mid(0, CUT2, hop1_a)
    hop2_a = hop(sent_a[0], sent_a[1])
    sent_b, sh_b, wide_b = mid(CUT2, PAIRS - CUT2, hop1)
    hop2_b = hop(sent_b[0], sent_b[1])
    hop2 = hop2_a + hop2_b

    own, other = call(
        grad_kernel,
        [VMEM] * 17,
        [shape(PIECES, F32), shape(PIECES, F32)],
        [WIDE, VALUES, FRAME1, pltpu.VMEM(ACC, F32), pltpu.VMEM(TACC, F32), pltpu.VMEM((2, HALF, CH), F32)],
        "grads",
    )(info, *hop1, x, g, s, sent_a, sent_b, sh_a, sh_b, wide_a, wide_b, acc, tacc, tb)

    other = call(hold_kernel, [ANY] * 3, [shape(PIECES, F32)], [], "hold", [ANY], {2: 0})(*hop2_a, other)[0]
    chunks = split_call("core_sum", 2, SIDE, PIECES[1:], 0, BF16)(own, lax.ppermute(other, "dp", swap))
    frames = [pltpu.HBM((2,) + FRAME, BF16), shape((8, CH), F32)]
    early_out, done_a = call(
        early_out_kernel, [VMEM] * 6 + [ANY], frames, [TAPS, FRAME1, SEM], "early_out", [ANY, VMEM]
    )(info, x, s, sh_a, sh_b, tf, chunks[0])
    early_in, done_b = call(
        early_in_kernel, [VMEM] * 9 + [ANY], frames, [TAPS, WIDE, FRAME1, SEM], "early_in", [ANY, VMEM]
    )(info, x, g, *hop1, wb, tb, chunks[0])
    part = split_call("x_sum", SIDE, 1, PIECES[1:], 2, BF16)(*to_sum(chunks, "x"), done_a, done_b)[0]
    block_out, done_c = call(
        output_kernel, [VMEM] * 8 + [ANY], frames, [FRAME1, SEM], "output", [ANY, VMEM], {8: 0}
    )(info, x, s, *hop2, tf, in_hbm(early_out))
    part = split_call("y_sum", SIDE, 1, PIECES[1:], 1, BF16)(*gather(part, "y"), done_c)[0]

    def input_half(first, so_far):
        return call(
            functools.partial(input_kernel, first=first),
            [VMEM] * 9 + [ANY],
            frames,
            [WIDE, FRAME1, SEM],
            "input_grad",
            [ANY, VMEM],
            {9: 0},
        )(info, x, g, *hop2, wb, tb, in_hbm(so_far))

    input_grad, done_d = input_half(0, early_in)
    part = split_call("z_sum", SIDE, 1, PIECES[1:], 1, BF16)(*gather(part, "z"), done_d)[0]
    input_grad, done_e = input_half(PAIRS // 2, input_grad)
    own = stack_call("x_stack", PIECES, 1)(*gather(part, "x"), done_e)
    theirs = lax.ppermute(own, "dp", swap)
    spatial_grad, temporal_grad = call(
        place_kernel, [VMEM, VMEM, VMEM], [shape((9 * CH, CH), F32), shape((3 * CH, CH), F32)], [], "place"
    )(info, own, theirs)
    return (
        block_out.reshape(latents.shape),
        input_grad.reshape(latents.shape),
        spatial_grad.reshape(3, 3, CH, CH),
        temporal_grad.reshape(3, CH, CH),
    )


def solution(mesh):
    chips = Mesh(mesh.devices.reshape(2, SIDE, SIDE, SIDE), ("dp", "x", "y", "z"))
    held = P(("dp", "x", "y", "z"), None, None, None)
    return jax.shard_map(
        local,
        mesh=chips,
        in_specs=(held, held, P("dp", None), P(), P()),
        out_specs=(held, held, P(), P()),
        check_vma=False,
    )
```

```python
import functools

import jax
import jax.numpy as jnp
from jax import lax
from jax.experimental import pallas as pl
from jax.experimental.pallas import tpu as pltpu
from jax.sharding import Mesh
from jax.sharding import PartitionSpec as P

FRAMES = 9
CLIPS = 8
CH = 128
ROWS = 64
COLS = 64
N_SP = 64
SIDE = 4
PAIRS = ROWS // 2
F32 = jnp.float32
BF16 = jnp.bfloat16
VMEM_BYTES = 24 * 1024 * 1024
SCALE = float(2 * CLIPS * FRAMES * ROWS * COLS) ** (-0.5)
HALF = 6 * CH
PIECE = HALF // SIDE

COUNT, EVEN, BACK1, NEXT1, NEXT2, LBACK1, LBACK2, LNEXT1, CORE, AT_X = range(10)
INFO = (8, 128)

FILL = 8
MID = 16
FULL = 32
CUT1 = 16
CUT2 = 15


def dot(a, b):
    return jnp.dot(a, b, preferred_element_type=F32)


def dot_t(a, b):
    return lax.dot_general(a, b, (((0,), (0,)), ((), ())), preferred_element_type=F32)


def steps(block, body):
    def one(n, _):
        body(n * block)
        return 0

    lax.fori_loop(0, PAIRS // block, one, 0)


def clear_edges(wide):
    wide[0, :, 0 : 3 * CH] = jnp.zeros((COLS, 3 * CH), BF16)
    wide[PAIRS, :, 3 * CH : 6 * CH] = jnp.zeros((COLS, 3 * CH), BF16)


def put_row(wide, t, half, a):
    col = lax.broadcasted_iota(jnp.int32, a.shape, 1)
    before = jnp.where(col == 0, 0.0, pltpu.roll(a, 1, 1))
    after = jnp.where(col == COLS - 1, 0.0, pltpu.roll(a, COLS - 1, 1))
    at = pl.ds(t + half, a.shape[0])
    base = 0 if half else 3 * CH
    wide[at, :, base : base + CH] = before.astype(BF16)
    wide[at, :, base + CH : base + 2 * CH] = a.astype(BF16)
    wide[at, :, base + 2 * CH : base + 3 * CH] = after.astype(BF16)


def put_act(wide, t, half, x):
    x = x.astype(F32)
    put_row(wide, t, half, x * jax.nn.sigmoid(x))


def fill_act(wide, rows, first=0, count=PAIRS):
    for t in range(first, first + count, FILL):
        for half in range(2):
            put_act(wide, t, half, rows(t, FILL, half))


def windows(wide, t, block):
    low = wide[pl.ds(t, block)].reshape(block * COLS, 6 * CH)
    high = wide[pl.ds(t + 1, block)].reshape(block * COLS, 6 * CH)
    return low, high


def conv(wide, w_ref, t, block):
    low, high = windows(wide, t, block)
    return dot(low, w_ref[0 : 6 * CH, :]) + dot(high, w_ref[6 * CH : 12 * CH, :])


def conv_to(out_ref, wide, w_ref):
    def body(t):
        out_ref[pl.ds(t, FULL)] = conv(wide, w_ref, t, FULL).astype(BF16).reshape(FULL, COLS, 2 * CH)

    steps(FULL, body)


def pair(v):
    return jnp.concatenate([v[:, 0], v[:, 1]], axis=-1).reshape(v.shape[0] * COLS, 2 * CH)


def flat(v):
    return v.reshape(v.shape[0] * COLS, 2 * CH)


def add_spatial(acc, wide, v_ref):
    def body(t):
        low, high = windows(wide, t, FULL)
        v = flat(v_ref[pl.ds(t, FULL)])
        acc[:, 0 : 6 * CH] += dot_t(v, low)
        acc[:, 6 * CH : 12 * CH] += dot_t(v, high)

    steps(FULL, body)


def correlate(s, gs):
    total = None
    for half in range(2):
        a = s[:, :, half * CH : half * CH + CH].reshape(s.shape[0] * COLS, CH)
        b = gs(half)
        one = dot_t(a, b.reshape(s.shape[0] * COLS, b.shape[-1]))
        total = one if total is None else total + one
    return total


def copy_either(first, a, b, sem):
    @pl.when(first)
    def _():
        pltpu.make_async_copy(*a, sem).start()

    @pl.when(jnp.logical_not(first))
    def _():
        pltpu.make_async_copy(*b, sem).start()

    return pltpu.make_async_copy(*a, sem)


def is_two(info):
    return info[0, COUNT] == 2


def is_set(info, n):
    return info[0, n] == 1


def either(first, a, b):
    return lambda *at: jnp.where(first, a[at], b[at])


def halves(first, a, b, cut):
    parts = (either(first, a[0], b[0]), either(first, a[1], b[1]))

    def read(t, n, *at):
        found = []
        if t < cut:
            found.append(parts[0](pl.ds(t, min(n, cut - t)), *at))
        if t + n > cut:
            start = max(t, cut)
            found.append(parts[1](pl.ds(start - cut, t + n - start), *at))
        return found[0] if len(found) == 1 else jnp.concatenate(found, axis=0)

    return read


def prep_kernel(counts, x_hbm, g_hbm, info, high_ref, low_ref, sems):
    here = (lax.axis_index("x") * SIDE + lax.axis_index("y")) * SIDE + lax.axis_index("z")
    even = here % 2 == 0

    rows = pl.ds(0, CUT1)

    def put(source, slot, for_high, n):
        return [copy_either(for_high, (source.at[slot, rows], high_ref), (source.at[slot, rows], low_ref), sems.at[n])]

    copies = put(g_hbm, 0, even, 0)
    c = counts[...].astype(F32)
    order = lax.broadcasted_iota(jnp.int32, c.shape, 1)
    start = jnp.sum(jnp.where(order < here, c, 0.0)).astype(jnp.int32)
    count = jnp.sum(jnp.where(order == here, c, 0.0)).astype(jnp.int32)
    copies += put(x_hbm, jnp.where(count == 2, 1, 0), jnp.logical_not(even), 1)
    first = start % FRAMES
    second = (first + 1) % FRAMES
    final = FRAMES - 1
    values = {
        COUNT: count,
        EVEN: even.astype(jnp.int32),
        BACK1: (first >= 1).astype(jnp.int32),
        NEXT1: (first + 1 <= final).astype(jnp.int32),
        NEXT2: (first + 2 <= final).astype(jnp.int32),
        LBACK1: (second >= 1).astype(jnp.int32),
        LBACK2: (second >= 2).astype(jnp.int32),
        LNEXT1: (second + 1 <= final).astype(jnp.int32),
        CORE: lax.axis_index("dp"),
        AT_X: lax.axis_index("x"),
    }
    lane = lax.broadcasted_iota(jnp.int32, INFO, 1)
    found = jnp.zeros(INFO, jnp.int32)
    for n, value in values.items():
        found = jnp.where(lane == n, value, found)
    info[...] = found
    for c in copies:
        c.wait()


def prep2_kernel(info, x_hbm, g_hbm, high_ref, low_ref, sems):
    even = is_set(info, EVEN)
    last = jnp.where(is_two(info), 1, 0)
    rows = pl.ds(CUT1, PAIRS - CUT1)
    down, up = g_hbm.at[0, rows], x_hbm.at[last, rows]
    copies = [
        copy_either(even, (down, high_ref), (down, low_ref), sems.at[0]),
        copy_either(even, (up, low_ref), (up, high_ref), sems.at[1]),
    ]
    for c in copies:
        c.wait()


def forward_kernel(info, x_ref, g_ref, w_ref, tw_ref, s_ref, acc, tacc, wf, wb, tf, tb, wide, v_ref, mw):
    zero = jnp.zeros((CH, CH), BF16)
    for a in range(4):
        for q in range(3):
            rows = slice((a * 3 + q) * CH, (a * 3 + q + 1) * CH)
            for b in range(2):
                lanes = slice(b * CH, b * CH + CH)
                inside = 0 <= a - b <= 2
                wf[rows, lanes] = w_ref[a - b, q] if inside else zero
                wb[rows, lanes] = w_ref[2 - (a - b), 2 - q].T if inside else zero
    for k in range(3):
        for a in range(2):
            rows = slice((2 * k + a) * CH, (2 * k + a + 1) * CH)
            for b in range(2):
                lanes = slice(b * CH, b * CH + CH)
                tf[rows, lanes] = tw_ref[k] if a == b else zero
                tb[rows, lanes] = tw_ref[k].T if a == b else zero

    acc[...] = jnp.zeros_like(acc)
    tacc[...] = jnp.zeros_like(tacc)
    clear_edges(wide)
    mw[0 : 2 * CH] = tb[0 : 2 * CH]

    def slot(j, _):
        keep = jnp.logical_and(j == 0, jnp.logical_and(is_two(info), is_set(info, NEXT1)))
        mw[2 * CH : 4 * CH] = jnp.where(keep, tb[2 * CH : 4 * CH], jnp.zeros((2 * CH, 2 * CH), BF16))
        fill_act(wide, lambda t, n, half: x_ref[j, pl.ds(t, n), half])
        conv_to(s_ref.at[j], wide, wf)

        def upstream(t):
            at = pl.ds(t, MID)
            both = jnp.concatenate([pair(g_ref[j, at]), pair(g_ref[1, at])], axis=-1)
            v_ref[at] = dot(both, mw[...]).astype(BF16).reshape(MID, COLS, 2 * CH)

        steps(MID, upstream)
        add_spatial(acc, wide, v_ref)
        found = correlate(s_ref[j], lambda half: jnp.concatenate([g_ref[j, :, half], g_ref[1, :, half]], axis=-1))
        tacc[:, 0:CH] += found[:, 0:CH]
        tacc[:, CH : 2 * CH] += jnp.where(keep, found[:, CH : 2 * CH], 0.0)
        return 0

    lax.fori_loop(0, info[0, COUNT], slot, 0)


def mid_kernel(info, *refs, first, count):
    *hops, s, g, wf, tf, tb, sent, sh, wide, mw = refs
    if len(hops) == 2:
        hops = hops * 2
    two = is_two(info)
    even = is_set(info, EVEN)
    back = is_set(info, BACK1)
    before = halves(even, hops[0::2], hops[1::2], CUT1)
    after = halves(even, hops[1::2], hops[0::2], CUT1)
    end = first + count
    if first == 0:
        wide[0, :, 0 : 3 * CH] = jnp.zeros((COLS, 3 * CH), BF16)
    else:
        put_act(wide, -1, 1, before(first - 1, 1, 1))
    for t in range(first, end, FILL):
        n = min(FILL, end - t)
        for half in range(2):
            put_act(wide, t - first, half, before(t, n, half))
    if end == PAIRS:
        wide[count, :, 3 * CH : 6 * CH] = jnp.zeros((COLS, 3 * CH), BF16)
    else:
        put_act(wide, count, 0, before(end, 1, 0))
    sh[...] = conv(wide, wf, 0, count).astype(BF16).reshape(count, COLS, 2 * CH)

    down = jnp.where(even, 0, 1)
    at = pl.ds(first, count)
    nothing = jnp.zeros((2 * CH, 2 * CH), BF16)
    mw[0 : 2 * CH] = jnp.where(back, tb[2 * CH : 4 * CH], nothing)
    mw[2 * CH : 4 * CH] = jnp.where(jnp.logical_and(back, is_set(info, NEXT1)), tb[4 * CH : 6 * CH], nothing)
    v = jnp.concatenate([pair(g[0, at]), pair(jnp.where(two, g[1, at], after(first, count)))], axis=-1)
    sent[down] = dot(v, mw[...]).astype(BF16).reshape(count, COLS, 2 * CH)

    keep1 = jnp.where(two, info[0, LNEXT1], info[0, NEXT1]) == 1
    keep2 = jnp.logical_and(keep1, jnp.where(two, info[0, LBACK1], info[0, BACK1]) == 1)
    mw[0 : 2 * CH] = jnp.where(keep1, tf[2 * CH : 4 * CH], nothing)
    mw[2 * CH : 4 * CH] = jnp.where(keep2, tf[4 * CH : 6 * CH], nothing)
    v = jnp.concatenate([flat(jnp.where(two, s[1, at], s[0, at])), flat(jnp.where(two, s[0, at], sh[...]))], axis=-1)
    sent[1 - down] = dot(v, mw[...]).astype(BF16).reshape(count, COLS, 2 * CH)


def grad_kernel(
    info, high_a, low_a, high_b, low_b, x, g, s, sent_a, sent_b, sh_a, sh_b, wide_a, wide_b, acc_in, tacc_in, tb,
    own_ref, other_ref, wide, v, gn, acc, tacc, both
):
    two = is_two(info)
    even = is_set(info, EVEN)
    back = is_set(info, BACK1)
    cross = jnp.logical_and(back, is_set(info, NEXT1))
    after = halves(even, (low_a, low_b), (high_a, high_b), CUT1)
    down = jnp.where(even, 0, 1)
    acc[...] = acc_in[...]
    tacc[...] = tacc_in[...]
    for t in range(0, PAIRS, FILL):
        gn[pl.ds(t, FILL)] = after(t, FILL)
    for t, sent, sh, part in ((0, sent_a, sh_a, wide_a), (CUT2, sent_b, sh_b, wide_b)):
        n = sh.shape[0]
        at = pl.ds(t, n)

        def two_frames(half, at=at):
            return jnp.concatenate([g[0, at, half], jnp.where(two, g[1, at, half], gn[at, half])], axis=-1)

        found = correlate(sh[...], two_frames)
        tacc[:, CH : 2 * CH] += jnp.where(back, found[:, 0:CH], 0.0)
        tacc[:, 2 * CH : 3 * CH] += jnp.where(cross, found[:, CH : 2 * CH], 0.0)
        low, high = windows(part, 0, n)
        value = flat(sent[down])
        acc[:, 0 : 6 * CH] += dot_t(value, low)
        acc[:, 6 * CH : 12 * CH] += dot_t(value, high)

    @pl.when(jnp.logical_and(two, is_set(info, NEXT2)))
    def _():
        clear_edges(wide)
        fill_act(wide, lambda t, n, half: x[0, pl.ds(t, n), half])

        def up(t):
            at = pl.ds(t, MID)
            v[at] = dot(pair(gn[at]), tb[4 * CH : 6 * CH]).astype(BF16).reshape(MID, COLS, 2 * CH)

        steps(MID, up)
        add_spatial(acc, wide, v)
        tacc[:, 2 * CH : 3 * CH] += correlate(s[0], lambda half: gn[:, half])

    at_x, core = info[0, AT_X], info[0, CORE]
    for p in range(3):
        for q in range(3):
            first = (p * 3 + q) * CH
            second = ((p + 1) * 3 + q) * CH
            found = acc[0:CH, first : first + CH] + acc[CH : 2 * CH, second : second + CH]
            n = p * 3 + q
            both[n // 6, (n % 6) * CH : (n % 6 + 1) * CH] = found.T * SCALE
    for k in range(3):
        both[1, (3 + k) * CH : (4 + k) * CH] = tacc[:, k * CH : k * CH + CH] * SCALE
    for i in range(SIDE):
        source = pl.ds(pl.multiple_of(lax.rem(at_x + i, SIDE) * PIECE, PIECE), PIECE)
        own_ref[i] = both[core, source]
        other_ref[i] = both[1 - core, source]


def add_x(x, slot, out, to, sem, t, n, value):
    at = pl.ds(t, n)
    value = value.astype(BF16).astype(F32).reshape(n, COLS, 2 * CH)
    for half in range(2):
        out[at, half] = (x[slot, at, half].astype(F32) + value[:, :, half * CH : half * CH + CH]).astype(BF16)
    pltpu.make_async_copy(out.at[at], to.at[at], sem).start()


def mask_taps(mw, taps, keep1, keep2):
    nothing = jnp.zeros((2 * CH, 2 * CH), BF16)
    mw[0 : 2 * CH] = taps[0 : 2 * CH]
    mw[2 * CH : 4 * CH] = jnp.where(keep1, taps[2 * CH : 4 * CH], nothing)
    mw[4 * CH : 6 * CH] = jnp.where(keep2, taps[4 * CH : 6 * CH], nothing)


def put_upstream(wide, t, n, value):
    value = value.reshape(n, COLS, 2 * CH)
    for half in range(2):
        put_row(wide, t, half, value[:, :, half * CH : half * CH + CH])


def input_rows(wide, wb, x, g, slot, out, to, sem, first, count):
    at = pl.ds(first, count)
    back = conv(wide, wb, first, count).reshape(count, COLS, 2 * CH)
    for half in range(2):
        xv = x[slot, at, half].astype(F32)
        sig = jax.nn.sigmoid(xv)
        b = back[:, :, half * CH : half * CH + CH]
        out[at, half] = (g[slot, at, half].astype(F32) + b * (sig * (1.0 + xv * (1.0 - sig)))).astype(BF16)
    pltpu.make_async_copy(out.at[at], to.at[at], sem).start()


def early_out_kernel(info, x, s, sh_a, sh_b, tf, after, out_any, token, mw, out, sem):
    to = out_any.at[1]

    @pl.when(is_two(info))
    def _():
        mask_taps(mw, tf, is_set(info, LBACK1), is_set(info, LBACK2))
        for t, sh in ((0, sh_a), (CUT2, sh_b)):
            n = sh.shape[0]
            at = pl.ds(t, n)
            v = jnp.concatenate([flat(s[1, at]), flat(s[0, at]), flat(sh[...])], axis=-1)
            add_x(x, 1, out, to, sem, t, n, dot(v, mw[...]))

    @pl.when(jnp.logical_not(is_two(info)))
    def _():
        out[...] = jnp.zeros_like(out)
        pltpu.make_async_copy(out, to, sem).start()

    token[...] = jnp.zeros_like(token)
    pltpu.make_async_copy(out, to, sem).wait()


def early_in_kernel(info, x, g, high_a, low_a, high_b, low_b, wb, tb, after, out_any, token, mw, wide, out, sem):
    two = is_two(info)
    coming = halves(is_set(info, EVEN), (low_a, low_b), (high_a, high_b), CUT1)

    @pl.when(two)
    def _():
        mask_taps(mw, tb, is_set(info, NEXT1), is_set(info, NEXT2))
        clear_edges(wide)
        for t in range(0, PAIRS, FILL):
            at = pl.ds(t, FILL)
            v = jnp.concatenate([pair(g[0, at]), pair(g[1, at]), pair(coming(t, FILL))], axis=-1)
            put_upstream(wide, t, FILL, dot(v, mw[...]))
        for t in range(0, PAIRS, MID):
            input_rows(wide, wb, x, g, 0, out, out_any.at[0], sem, t, MID)

    @pl.when(jnp.logical_not(two))
    def _():
        out[...] = jnp.zeros_like(out)
        pltpu.make_async_copy(out, out_any.at[1], sem).start()

    token[...] = jnp.zeros_like(token)
    pltpu.make_async_copy(out, out_any.at[1], sem).wait()


def output_kernel(info, x, s, high_a, low_a, high_b, low_b, tf, early, out_any, token, out, sem):
    ahead = halves(is_set(info, EVEN), (high_a, high_b), (low_a, low_b), CUT2)
    to = out_any.at[0]
    for t, n in ((0, CUT2), (CUT2, PAIRS - CUT2)):
        value = dot(flat(s[0, pl.ds(t, n)]), tf[0 : 2 * CH]) + flat(ahead(t, n)).astype(F32)
        add_x(x, 0, out, to, sem, t, n, value)
    token[...] = jnp.zeros_like(token)
    pltpu.make_async_copy(out, to, sem).wait()


def input_kernel(info, x, g, high_a, low_a, high_b, low_b, wb, tb, early, out_any, token, wide, out, sem, *, first):
    last = jnp.where(is_two(info), 1, 0)
    share = halves(is_set(info, EVEN), (low_a, low_b), (high_a, high_b), CUT2)
    to = out_any.at[last]
    clear_edges(wide)
    done = max(first - 1, 0)
    end = min(first + MID + 1, PAIRS)
    while done < end:
        n = min(FILL - done % FILL, end - done)
        value = dot(pair(g[last, pl.ds(done, n)]), tb[0 : 2 * CH]) + flat(share(done, n)).astype(F32)
        put_upstream(wide, done, n, value)
        done += n
    input_rows(wide, wb, x, g, last, out, to, sem, first, MID)
    token[...] = jnp.zeros_like(token)
    rows = pl.ds(first, MID)
    pltpu.make_async_copy(out.at[rows], to.at[rows], sem).wait()


def hold_kernel(*refs):
    pass


def place_kernel(info, mine, theirs, spatial, temporal_out):
    at_x, core = info[0, AT_X], info[0, CORE]
    for half in range(2):
        for i in range(SIDE):
            n = lax.rem(at_x + SIDE - i, SIDE)
            piece = jnp.where(core == half, mine[n], theirs[n]).astype(F32)
            row = half * HALF + i * PIECE
            if row < 9 * CH:
                spatial[row : row + PIECE] = piece
            else:
                temporal_out[row - 9 * CH : row - 9 * CH + PIECE] = piece


FRAME = (PAIRS, 2, COLS, CH)
S_SHAPE = (PAIRS, COLS, 2 * CH)
WIDE = pltpu.VMEM((PAIRS + 1, COLS, 6 * CH), BF16)
VALUES = pltpu.VMEM(S_SHAPE, BF16)
W_SHAPE = (12 * CH, 2 * CH)
T_SHAPE = (6 * CH, 2 * CH)
TAPS = pltpu.VMEM(T_SHAPE, BF16)
TAPS2 = pltpu.VMEM((4 * CH, 2 * CH), BF16)
ACC = (2 * CH, 12 * CH)
TACC = (CH, 3 * CH)
PIECES = (SIDE, PIECE, CH)
VMEM = pl.BlockSpec(memory_space=pltpu.VMEM)
ANY = pl.BlockSpec(memory_space=pl.ANY)
HBM = pl.BlockSpec(memory_space=pltpu.HBM)
FRAME1 = pltpu.VMEM(FRAME, BF16)
SEM = pltpu.SemaphoreType.DMA
def shape(s, d=BF16):
    return jax.ShapeDtypeStruct(s, d)


def in_hbm(value):
    return pltpu.with_memory_space_constraint(value, pltpu.HBM)


def call(kernel, in_specs, outs, scratch, name, out_specs=None, aliases=None):
    return pl.pallas_call(
        kernel,
        in_specs=in_specs,
        out_specs=out_specs or [VMEM] * len(outs),
        out_shape=outs,
        scratch_shapes=scratch,
        input_output_aliases=aliases or {},
        compiler_params=pltpu.CompilerParams(vmem_limit_bytes=VMEM_BYTES),
        cost_estimate=pl.CostEstimate(flops=1, transcendentals=0, bytes_accessed=1),
        name=name,
    )


def shifts(value, axis, k):
    return lax.ppermute(value, axis, [(i, (i + k) % SIDE) for i in range(SIDE)])


def to_sum(parts, axis):
    return [parts[0]] + [shifts(parts[k], axis, k) for k in range(1, SIDE)]


def gather(part, axis):
    return [part] + [shifts(part, axis, k) for k in range(1, SIDE)]


def split_call(name, n_sum, n_out, out, n_after=0, kind=F32):
    def kernel(*refs):
        ins, outs = refs[:n_sum], refs[n_sum + n_after :]
        for n, out_ref in enumerate(outs):
            v = [(r[n] if n_out > 1 else r[...]).astype(F32) for r in ins]
            total = v[0] + v[1] if n_sum == 2 else (v[0] + v[2]) + (v[1] + v[3])
            out_ref[...] = total.astype(kind)

    return call(kernel, [VMEM] * n_sum + [ANY] * n_after, [shape(out, kind)] * n_out, [], name)


def stack_call(name, out, n_after):
    def kernel(*refs):
        for n in range(SIDE):
            refs[-1][n] = refs[n][...]

    run = call(kernel, [VMEM] * SIDE + [ANY] * n_after, [shape(out)], [], name)
    return lambda *a: run(*a)[0]


def local(latents, cotangent, frame_counts, spatial_weight, temporal_weight):
    axes = ("x", "y", "z")
    x = latents.reshape((2,) + FRAME)
    g = cotangent.reshape((2,) + FRAME)
    lows = range(0, N_SP, 2)
    low = [(i, i + 1) for i in lows] + [(i + 1, i) for i in lows]
    high = [(i + 1, (i + 2) % N_SP) for i in lows] + [((i + 2) % N_SP, i + 1) for i in lows]
    swap = [(0, 1), (1, 0)]

    top, bottom = shape((CUT1, 2, COLS, CH)), shape((PAIRS - CUT1, 2, COLS, CH))
    x_hbm, g_hbm = in_hbm(x), in_hbm(g)
    info, *sent1 = call(
        prep_kernel, [VMEM, HBM, HBM], [shape(INFO, jnp.int32), top, top], [SEM((2,))], "prep", [VMEM, ANY, ANY]
    )(frame_counts, x_hbm, g_hbm)
    sent2 = call(prep2_kernel, [VMEM, HBM, HBM], [bottom, bottom], [SEM((2,))], "prep2", [ANY, ANY])(info, x_hbm, g_hbm)

    def hop(for_high, for_low):
        return lax.ppermute(for_high, axes, high), lax.ppermute(for_low, axes, low)

    hop1_a = hop(*sent1)
    hop1_b = hop(*sent2)
    hop1 = hop1_a + hop1_b

    s, acc, tacc, wf, wb, tf, tb = call(
        forward_kernel,
        [VMEM] * 5,
        [shape((2,) + S_SHAPE), shape(ACC, F32), shape(TACC, F32), shape(W_SHAPE), shape(W_SHAPE), shape(T_SHAPE), shape(T_SHAPE)],
        [WIDE, VALUES, TAPS2],
        "forward",
    )(info, x, g, spatial_weight, temporal_weight)

    def mid(first, count, hops):
        return call(
            functools.partial(mid_kernel, first=first, count=count),
            [VMEM] * (6 + len(hops)),
            [shape((2, count) + S_SHAPE[1:]), shape((count,) + S_SHAPE[1:]), shape((count + 1, COLS, 6 * CH))],
            [TAPS2],
            "mid",
        )(info, *hops, s, g, wf, tf, tb)

    sent_a, sh_a, wide_a = mid(0, CUT2, hop1_a)
    hop2_a = hop(sent_a[0], sent_a[1])
    sent_b, sh_b, wide_b = mid(CUT2, PAIRS - CUT2, hop1)
    hop2_b = hop(sent_b[0], sent_b[1])
    hop2 = hop2_a + hop2_b

    own, other = call(
        grad_kernel,
        [VMEM] * 17,
        [shape(PIECES, F32), shape(PIECES, F32)],
        [WIDE, VALUES, FRAME1, pltpu.VMEM(ACC, F32), pltpu.VMEM(TACC, F32), pltpu.VMEM((2, HALF, CH), F32)],
        "grads",
    )(info, *hop1, x, g, s, sent_a, sent_b, sh_a, sh_b, wide_a, wide_b, acc, tacc, tb)

    other = call(hold_kernel, [ANY] * 3, [shape(PIECES, F32)], [], "hold", [ANY], {2: 0})(*hop2_a, other)[0]
    chunks = split_call("core_sum", 2, SIDE, PIECES[1:], 0, BF16)(own, lax.ppermute(other, "dp", swap))
    frames = [pltpu.HBM((2,) + FRAME, BF16), shape((8, CH), F32)]
    early_out, done_a = call(
        early_out_kernel, [VMEM] * 6 + [ANY], frames, [TAPS, FRAME1, SEM], "early_out", [ANY, VMEM]
    )(info, x, s, sh_a, sh_b, tf, chunks[0])
    early_in, done_b = call(
        early_in_kernel, [VMEM] * 9 + [ANY], frames, [TAPS, WIDE, FRAME1, SEM], "early_in", [ANY, VMEM]
    )(info, x, g, *hop1, wb, tb, chunks[0])
    part = split_call("x_sum", SIDE, 1, PIECES[1:], 2, BF16)(*to_sum(chunks, "x"), done_a, done_b)[0]
    block_out, done_c = call(
        output_kernel, [VMEM] * 8 + [ANY], frames, [FRAME1, SEM], "output", [ANY, VMEM], {8: 0}
    )(info, x, s, *hop2, tf, in_hbm(early_out))
    part = split_call("y_sum", SIDE, 1, PIECES[1:], 1, BF16)(*gather(part, "y"), done_c)[0]

    def input_half(first, so_far):
        return call(
            functools.partial(input_kernel, first=first),
            [VMEM] * 9 + [ANY],
            frames,
            [WIDE, FRAME1, SEM],
            "input_grad",
            [ANY, VMEM],
            {9: 0},
        )(info, x, g, *hop2, wb, tb, in_hbm(so_far))

    input_grad, done_d = input_half(0, early_in)
    part = split_call("z_sum", SIDE, 1, PIECES[1:], 1, BF16)(*gather(part, "z"), done_d)[0]
    input_grad, done_e = input_half(PAIRS // 2, input_grad)
    own = stack_call("x_stack", PIECES, 1)(*gather(part, "x"), done_e)
    theirs = lax.ppermute(own, "dp", swap)
    spatial_grad, temporal_grad = call(
        place_kernel, [VMEM, VMEM, VMEM], [shape((9 * CH, CH), F32), shape((3 * CH, CH), F32)], [], "place"
    )(info, own, theirs)
    return (
        block_out.reshape(latents.shape),
        input_grad.reshape(latents.shape),
        spatial_grad.reshape(3, 3, CH, CH),
        temporal_grad.reshape(3, CH, CH),
    )


def solution(mesh):
    chips = Mesh(mesh.devices.reshape(2, SIDE, SIDE, SIDE), ("dp", "x", "y", "z"))
    held = P(("dp", "x", "y", "z"), None, None, None)
    return jax.shard_map(
        local,
        mesh=chips,
        in_specs=(held, held, P("dp", None), P(), P()),
        out_specs=(held, held, P(), P()),
        check_vma=False,
    )
```
